1024 devices in a mesh: pix: 64 (over z, y), lev: 8 (over x_hi, core), head: 2 (over x_lo).
Axes of the slice: x: 8 (x_hi: 4, x_lo: 2; x = x_hi * 2 + x_lo), y: 8, z: 8, core: 2. Of those that a mesh axis runs over, the one named last changes fastest.
Arguments:
- fields: bfloat16 [16, 16384, 512], P('lev', 'pix'), may hold values from -6 to 6
- window_qkv: bfloat16 [3, 512, 512], P(None, None, 'head'), may hold values from -1 to 1
- window_out: bfloat16 [512, 512], P('head'), may hold values from -0.25 to 0.25
- level_embed: bfloat16 [16, 512], replicated, may hold values from -6 to 6
- level_order: int32 [16], replicated, may hold values from 0 to 15, each once
- column_qkv: bfloat16 [3, 512, 512], P(None, None, 'head'), may hold values from -1 to 1
- column_out: bfloat16 [512, 512], P('head'), may hold values from -0.25 to 0.25
Outputs:
- layer_out: bfloat16 [16, 16384, 512], P('head', ('pix', 'lev'))
The draws below stay inside these ranges and needn't reach their ends.
All inputs are finite; a program needn't handle non-finite values.
Results may differ from the reference program's by a relative error of at most 0.018.
Values may be sent and summed in bfloat16 or wider, within the bound.
A program may use at most 32 MiB of HBM per device.

```python
import jax
import jax.numpy as jnp
from jax import lax

D = 512
HEADS = 8
HEAD_DIM = 64
LEVELS = 16
PIXELS = 16384
WINDOW = 1024
N_HEAD = 2


def draw_fields(key, part):
    key = jax.random.fold_in(key, 11)
    values = jax.random.normal(key, (LEVELS, PIXELS, D), jnp.float32)
    return jnp.clip(values, -6.0, 6.0).astype(jnp.bfloat16)


def attention_weights(key, strength):
    base_key, scale_key = jax.random.split(key)
    base = jax.random.normal(base_key, (3, D, D), jnp.float32)
    exponent = jax.random.uniform(scale_key, (HEADS,), jnp.float32)
    head_scale = jnp.repeat(strength ** exponent, HEAD_DIM)[None, :]
    query_part = base[0] * head_scale
    key_part = base[1] * head_scale
    stacked = jnp.stack([query_part, key_part, base[2]]) / jnp.sqrt(jnp.float32(D))
    return jnp.clip(stacked, -1.0, 1.0).astype(jnp.bfloat16)


def draw_window_qkv(key, part):
    key = jax.random.fold_in(key, 23)
    return attention_weights(key, 1.0)


def draw_column_qkv(key, part):
    key = jax.random.fold_in(key, 37)
    return attention_weights(key, 1.0)


def shard_levels(rng, shape, cuts, low, high):
    level, own = 1.0, jax.random.fold_in(rng, 6)
    for position, parts in cuts:
        steps = jnp.exp(jax.random.uniform(jax.random.fold_in(own, position), (parts,), jnp.float32, low / len(cuts), high / len(cuts)))
        level = level * jnp.repeat(steps, shape[position] // parts).reshape([-1 if axis == position else 1 for axis in range(len(shape))])
    return level


def centred(stream_key, dims, spread, reach, cuts=(), held_as=jnp.bfloat16):
    level = shard_levels(stream_key, dims, cuts, -0.22, 0.18) if cuts else 1.0
    values = jax.random.normal(stream_key, dims, jnp.float32) * spread * level
    return jnp.minimum(jnp.maximum(values, -reach), reach).astype(held_as)


def setup_inputs(seed: int = 0) -> dict:
    streams_of = jax.random.split(jax.random.key(seed), 8)
    fields = draw_fields(jax.random.fold_in(streams_of[7], 71), 0)
    window_qkv = draw_window_qkv(jax.random.fold_in(streams_of[7], 71), 0)
    window_out = centred(streams_of[2], (D, D), D ** -0.5, 0.25, ((0, 2),))
    level_embed = centred(streams_of[3], (LEVELS, D), 1.0, 6.0)
    level_order = jax.random.permutation(streams_of[4], LEVELS).astype(jnp.int32)
    column_qkv = draw_column_qkv(jax.random.fold_in(streams_of[7], 71), 0)
    column_out = centred(streams_of[6], (D, D), D ** -0.5, 0.25, ((0, 2),))
    return dict(fields=fields, window_qkv=window_qkv, window_out=window_out, level_embed=level_embed, level_order=level_order, column_qkv=column_qkv, column_out=column_out)


epsilon = 1e-06

def normalize(values):
    return values * lax.rsqrt(lax.optimization_barrier(jnp.mean(values * values, axis=-1, keepdims=True)) + epsilon)

def attend(queries, keys_in, values, head_count):
    batch, length, features = queries.shape
    key_len = keys_in.shape[1]
    head_width = features // head_count
    query_heads = queries.reshape(batch, length, head_count, head_width).astype(jnp.float32)
    key_heads = keys_in.reshape(batch, key_len, head_count, head_width).astype(jnp.float32)
    value_heads = values.reshape(batch, key_len, head_count, head_width).astype(jnp.float32)
    scores = jnp.einsum('bqhd,bkhd->bhqk', query_heads, key_heads) * head_width ** (-0.5)
    top_score = lax.optimization_barrier(jnp.max(scores, axis=-1, keepdims=True))
    weights = jnp.exp(scores - top_score)
    totals = lax.optimization_barrier(jnp.sum(weights, axis=-1))
    rounded = lax.optimization_barrier(weights.astype(jnp.bfloat16)).astype(jnp.float32)
    output = jnp.einsum('bhqk,bkhd->bqhd', rounded, value_heads)
    output = output / jnp.transpose(totals, (0, 2, 1))[..., None]
    return output.reshape(batch, length, features).astype(jnp.bfloat16)

def project(rows, weight):
    return jnp.dot(rows, weight, preferred_element_type=jnp.float32).astype(jnp.bfloat16)

def grouped_sum(acts, weight):
    group = D // N_HEAD
    total = jnp.zeros((acts.shape[0], D), jnp.float32)
    for index in range(N_HEAD):
        piece = jnp.dot(acts[:, index * group:(index + 1) * group], weight[index * group:(index + 1) * group], preferred_element_type=jnp.float32)
        total = total + lax.optimization_barrier(piece.astype(jnp.bfloat16)).astype(jnp.float32)
    return total

def reference(fields, window_qkv, window_out, level_embed, level_order, column_qkv, column_out):
    rows = LEVELS * PIXELS
    normed = normalize(fields.astype(jnp.float32)).astype(jnp.bfloat16).reshape(rows, D)
    queries = project(normed, window_qkv[0])
    keys_all = project(normed, window_qkv[1])
    values = project(normed, window_qkv[2])
    blocks = LEVELS * (PIXELS // WINDOW)

    def one_window(items):
        return attend(items[0][None], items[1][None], items[2][None], HEADS)[0]
    window_att = lax.map(one_window, (queries.reshape(blocks, WINDOW, D), keys_all.reshape(blocks, WINDOW, D), values.reshape(blocks, WINDOW, D)))
    window_att = window_att.reshape(rows, D)
    mid = (fields.reshape(rows, D).astype(jnp.float32) + grouped_sum(window_att, window_out)).astype(jnp.bfloat16)
    onehot = (level_order[:, None] == jnp.arange(LEVELS, dtype=jnp.int32)[None, :]).astype(jnp.float32)
    embed_rows = jnp.dot(onehot, level_embed.astype(jnp.float32), precision=lax.Precision.HIGHEST)
    shifted = mid.reshape(LEVELS, PIXELS, D).astype(jnp.float32) + embed_rows[:, None, :]
    normed2 = normalize(shifted).astype(jnp.bfloat16).reshape(rows, D)
    queries2 = project(normed2, column_qkv[0]).reshape(LEVELS, PIXELS, D)
    keys2 = project(normed2, column_qkv[1]).reshape(LEVELS, PIXELS, D)
    values2 = project(normed2, column_qkv[2]).reshape(LEVELS, PIXELS, D)
    column_att = attend(jnp.transpose(queries2, (1, 0, 2)), jnp.transpose(keys2, (1, 0, 2)), jnp.transpose(values2, (1, 0, 2)), HEADS)
    column_att = jnp.transpose(column_att, (1, 0, 2)).reshape(rows, D)
    layer_out = (mid.astype(jnp.float32) + grouped_sum(column_att, column_out)).astype(jnp.bfloat16)
    return layer_out.reshape(LEVELS, PIXELS, D)
```

```python
import math

import jax
import jax.numpy as jnp
from jax import lax
from jax.experimental import pallas as pl
from jax.experimental.pallas import tpu as pltpu
from jax.sharding import PartitionSpec as P

MESH = pl.DeviceIdType.MESH
EPS = 1e-6
F32 = jnp.float32
BF16 = jnp.bfloat16
D = 512
HALF = 256
QSCALE = math.log2(math.e) / 8.0
LOW = -3.0e38


def normalize(values):
    return values * lax.rsqrt(jnp.mean(values * values, axis=-1, keepdims=True) + EPS)


def dot(a, b):
    return jnp.dot(a, b, preferred_element_type=F32)


def dot_t(a, b):
    return lax.dot_general(a, b, (((1,), (1,)), ((), ())), preferred_element_type=F32)


def quarter_of(xh, a, c):
    odd = xh % 2
    off = (1 - a) * (3 * c + (1 - c) * 2 * odd) + a * ((1 - c) + c * (2 - 2 * odd))
    return (xh + off) % 4


def quarter_owner(xh, q):
    odd = xh % 2
    off = (q - xh + 4) % 4
    is0 = jnp.where(off == 0, 1, 0)
    is1 = jnp.where(off == 1, 1, 0)
    is2 = jnp.where(off == 2, 1, 0)
    is3 = jnp.where(off == 3, 1, 0)
    a = is0 * odd + is1 + is2 * (1 - odd)
    c = is0 * odd + is2 * (1 - odd) + is3
    return a, c


def kernel(
    fields, wqkv, wout, embed, order, cqkv, cout,
    out,
    X, N, W, WO, CW, CO, EM,
    QM, KS, VS, OA, MA, MID, ATT,
    EB, M, N2, K2, V2, Q2,
    loc_sem, ys_sem, yr_sem, own_s, own_r, xs_sem, xr_sem,
    s1s_sem, s1r_sem, s2s_sem, s2r_sem, ws_sem, wr_sem, wfs_sem, wfr_sem,
    as_sem, ar_sem,
):
    pix = lax.axis_index("pix")
    lev = lax.axis_index("lev")
    a = lax.axis_index("head")
    i = pix % 4
    base = pix - i
    c = lev % 2
    xh = lev // 2
    level = 4 * xh + i
    cs = i // 2
    q = quarter_of(xh, a, c)
    q_sib = quarter_of(xh, a, 1 - c)
    q_par = quarter_of(xh, 1 - a, c)
    q_dia = quarter_of(xh, 1 - a, 1 - c)
    sib = (pix, 2 * xh + 1 - c, a)
    par = (pix, lev, 1 - a)
    xn = (xh + c * (2 * a - 1) + 4) % 4
    wpar = (pix, 2 * xn + c, 1 - a)
    e = ((i + 1) // 2) % 2
    j1 = i + 1 - 2 * (i % 2)
    opposite = (i + 2) % 4
    mirror = 3 - i
    j2 = opposite * (1 - e) + mirror * e
    j3 = mirror * (1 - e) + opposite * e

    def rows(quarter):
        return pl.ds(pl.multiple_of(quarter * 64, 64), 64)

    def remote(src, dst, ss, rs, dev):
        return pltpu.make_async_remote_copy(
            src_ref=src, dst_ref=dst, send_sem=ss, recv_sem=rs,
            device_id=dev, device_id_type=MESH,
        )

    local = [
        pltpu.make_async_copy(wqkv, W.at[0], loc_sem.at[0]),
        pltpu.make_async_copy(wout, WO.at[0], loc_sem.at[1]),
        pltpu.make_async_copy(cqkv, CW.at[0], loc_sem.at[2]),
        pltpu.make_async_copy(cout, CO.at[0], loc_sem.at[3]),
        pltpu.make_async_copy(embed, EM, loc_sem.at[4]),
    ]
    own_shard = pltpu.make_async_copy(fields.at[i % 2], X.at[i], loc_sem.at[5])

    @pl.when(c == cs)
    def _():
        own_shard.start()

    for copy in local:
        copy.start()

    barrier = pltpu.get_barrier_semaphore()

    def greet(dev):
        pl.semaphore_signal(barrier, inc=1, device_id=dev, device_id_type=MESH)

    for jj in (j1, j2, j3):
        greet((base + jj, 2 * xh + cs, a))
    greet(sib)
    greet(par)
    greet(wpar)
    for l in range(16):
        xs = l // 4
        sa, sc = quarter_owner(jnp.int32(xs), xh)
        src = (base + l % 4, 2 * xs + sc, sa)
        is_me = (i == l % 4) & (xh == xs) & (sc == c) & (sa == a)

        @pl.when(jnp.logical_not(is_me))
        def _():
            greet(src)

    n_y = jnp.where(c == cs, 2, 4)
    n_self = jnp.where(q == xh, 1, 0)
    pl.semaphore_wait(barrier, n_y + 3 + 16 - n_self)

    def y_send(b, cd):
        t = 2 * c + b
        quarter = quarter_of(xh, a, cd)
        return remote(
            fields.at[b, rows(quarter)], X.at[i, rows(quarter)],
            ys_sem.at[b, cd], yr_sem.at[i], (base + t, 2 * xh + cd, a),
        )

    for b in range(2):
        @pl.when(2 * c + b != i)
        def _():
            for cd in range(2):
                y_send(b, cd).start()

    own_send = remote(fields.at[i % 2], X.at[i], own_s, own_r, sib)

    @pl.when(c == cs)
    def _():
        own_send.start()

    wrow = pl.ds(pl.multiple_of(c * HALF, HALF), HALF)
    worow = pl.ds(pl.multiple_of(c * 128, 128), 128)
    w_srcs = [wqkv.at[:, wrow], wout.at[worow], cqkv.at[:, wrow], cout.at[worow]]
    w_dsts = [W.at[1, :, wrow], WO.at[1, worow], CW.at[1, :, wrow], CO.at[1, worow]]
    w_send = [remote(s, d, ws_sem.at[n], wr_sem.at[n], wpar) for n, (s, d) in enumerate(zip(w_srcs, w_dsts))]
    w_fwd = [remote(d, d, wfs_sem.at[n], wfr_sem.at[n], sib) for n, d in enumerate(w_dsts)]
    for n in range(4):
        w_send[n].start()

    def x_fwd(j):
        return remote(X.at[j, rows(q)], X.at[j, rows(q)], xs_sem.at[j], xr_sem.at[j], par)

    def s1_fwd(j):
        return remote(X.at[j, rows(q)], X.at[j, rows(q)], s1s_sem.at[j], s1r_sem.at[j], sib)

    def s2_fwd(j):
        return remote(X.at[j, rows(q_par)], X.at[j, rows(q_par)], s2s_sem.at[j], s2r_sem.at[j], sib)

    def y_recv(j):
        return remote(X.at[j, rows(q)], X.at[j, rows(q)], ys_sem.at[0, 0], yr_sem.at[j], par)

    def x_recv(j):
        return remote(X.at[j, rows(q_par)], X.at[j, rows(q_par)], xs_sem.at[j], xr_sem.at[j], par)

    def s1_recv(j):
        return remote(X.at[j, rows(q_sib)], X.at[j, rows(q_sib)], s1s_sem.at[j], s1r_sem.at[j], sib)

    def s2_recv(j):
        return remote(X.at[j, rows(q_dia)], X.at[j, rows(q_dia)], s2s_sem.at[j], s2r_sem.at[j], sib)

    lane = lax.broadcasted_iota(jnp.int32, (HALF, 128), 1)
    low_half = lane < 64

    @pl.when(c == cs)
    def _():
        own_shard.wait()

    @pl.when(c != cs)
    def _():
        own_send.wait_recv()

    N[i] = normalize(X[i].astype(F32)).astype(BF16)
    OA[...] = jnp.zeros_like(OA)
    MA[...] = jnp.full_like(MA, LOW)

    for jj in (j1, j2, j3):
        y_recv(jj).wait_recv()
        x_fwd(jj).start()
        s1_fwd(jj).start()

    local[0].wait()
    qrows = X[:, rows(q), :].reshape(HALF, D).astype(F32)
    nq = normalize(qrows).astype(BF16)

    def queries(g):
        qs = dot(nq, W[g, 0]) * QSCALE
        for h in range(4):
            pair = qs[:, 128 * (h // 2):128 * (h // 2) + 128]
            keep = low_half if h % 2 == 0 else jnp.logical_not(low_half)
            QM[4 * g + h] = jnp.where(keep, pair, 0.0).astype(BF16)

    queries(0)

    for jj in (j1, j2, j3):
        x_recv(jj).wait_recv()
        s2_fwd(jj).start()

    def attend(j, g):
        n = N[j]
        k = dot(n, W[g, 1]).astype(BF16)
        v = dot(n, W[g, 2])
        for p in range(2):
            KS[p] = k[:, 128 * p:128 * p + 128]
            vp = v[:, 128 * p:128 * p + 128]
            VS[2 * p] = jnp.where(low_half, vp, 1.0).astype(BF16)
            VS[2 * p + 1] = jnp.where(low_half, 1.0, vp).astype(BF16)
        for h in range(4):
            hh = 4 * g + h
            s = dot_t(QM[hh], KS[h // 2])
            top = jnp.max(s, axis=1, keepdims=True)
            old = MA[hh]
            new = jnp.maximum(old, top)
            wl = jnp.exp2(s[:, :128] - new).astype(BF16)
            wr = jnp.exp2(s[:, 128:] - new).astype(BF16)
            w = jnp.concatenate([wl, wr], axis=1)
            OA[hh] = OA[hh] * jnp.exp2(old - new) + dot(w, VS[h])
            MA[hh] = new

    attend(i, 0)
    for n in range(2):
        w_send[n].wait_recv()
        w_fwd[n].start()
    for n in range(2):
        w_fwd_in = remote(
            (W.at[1, :, pl.ds(pl.multiple_of((1 - c) * HALF, HALF), HALF)] if n == 0
             else WO.at[1, pl.ds(pl.multiple_of((1 - c) * 128, 128), 128)]),
            (W.at[1, :, pl.ds(pl.multiple_of((1 - c) * HALF, HALF), HALF)] if n == 0
             else WO.at[1, pl.ds(pl.multiple_of((1 - c) * 128, 128), 128)]),
            wfs_sem.at[n], wfr_sem.at[n], sib,
        )
        w_fwd_in.wait_recv()
    queries(1)
    attend(i, 1)

    def shard_step(s, carry):
        j = jnp.where(s == 0, j1, jnp.where(s == 1, j2, j3))
        s1_recv(j).wait_recv()
        s2_recv(j).wait_recv()
        N[j] = normalize(X[j].astype(F32)).astype(BF16)

        def group_step(g, inner):
            attend(j, g)
            return inner

        return lax.fori_loop(0, 2, group_step, carry)

    lax.fori_loop(0, 3, shard_step, 0)

    for p in range(4):
        oa, ob = OA[2 * p], OA[2 * p + 1]
        num = jnp.where(low_half, oa, ob)
        den = pltpu.roll(jnp.where(low_half, ob, oa), 64, 1)
        ATT[:, 128 * p:128 * p + 128] = (num / den).astype(BF16)

    local[1].wait()
    att = ATT[...]
    mid = qrows + dot(att[:, :HALF], WO[0]) + dot(att[:, HALF:], WO[1])
    MID[...] = mid.astype(BF16).reshape(8, 32, D)

    def a_send(n):
        j, ee, hd = n // 4, (n // 2) % 2, n % 2
        return remote(
            MID.at[n // 2], M.at[level], as_sem.at[n], ar_sem.at[level],
            (base + j, 2 * q + ee, hd),
        )

    def is_self(n):
        j, ee, hd = n // 4, (n // 2) % 2, n % 2
        return (i == j) & (q == xh) & (c == ee) & (a == hd)

    self_copy = pltpu.make_async_copy(MID.at[2 * i + c], M.at[level], loc_sem.at[5])
    for n in range(16):
        @pl.when(jnp.logical_not(is_self(n)))
        def _():
            a_send(n).start()

    @pl.when(q == xh)
    def _():
        @pl.when(is_self(4 * i + 2 * c + a))
        def _():
            self_copy.start()

    for n in range(2, 4):
        w_send[n].wait_recv()
        w_fwd[n].start()
    crow = pl.ds(pl.multiple_of((1 - c) * HALF, HALF), HALF)
    corow = pl.ds(pl.multiple_of((1 - c) * 128, 128), 128)
    remote(CW.at[1, :, crow], CW.at[1, :, crow], wfs_sem.at[2], wfr_sem.at[2], sib).wait_recv()
    remote(CO.at[1, corow], CO.at[1, corow], wfs_sem.at[3], wfr_sem.at[3], sib).wait_recv()
    for n in range(2, 5):
        local[n].wait()

    row = lax.broadcasted_iota(jnp.int32, (16, 16), 0)
    col = lax.broadcasted_iota(jnp.int32, (16, 16), 1)
    target = jnp.zeros((16, 16), jnp.int32)
    for l in range(16):
        target = jnp.where(row == l, order[l], target)
    onehot = jnp.where(col == target, 1.0, 0.0).astype(BF16)
    EB[...] = jnp.broadcast_to(dot(onehot, EM[...]).reshape(16, 1, D), (16, 8, D))

    def level_step(s, carry):
        step = jnp.where(s == 2, 3, jnp.where(s == 3, 2, s))
        xs = (xh + step) % 4
        for m in range(4):
            l = 4 * xs + m

            @pl.when(l == level)
            def _():
                @pl.when(q == xh)
                def _():
                    self_copy.wait()

                @pl.when(q != xh)
                def _():
                    a_recv(l).wait_recv()

            @pl.when(l != level)
            def _():
                a_recv(l).wait_recv()

            e32 = jnp.concatenate([EB[l]] * 4, axis=0)
            N2[l] = normalize(M[l].astype(F32) + e32).astype(BF16)
        four = N2[pl.ds(4 * xs, 4)].reshape(128, D)
        for g in range(2):
            lanes = slice(HALF * g, HALF * g + HALF)
            K2[pl.ds(4 * xs, 4), :, lanes] = dot(four, CW[g, 1]).astype(BF16).reshape(4, 32, HALF)
            V2[pl.ds(4 * xs, 4), :, lanes] = dot(four, CW[g, 2]).astype(BF16).reshape(4, 32, HALF)

        @pl.when(xs // 2 == a)
        def _():
            for g in range(2):
                lanes = slice(HALF * g, HALF * g + HALF)
                Q2[pl.ds(4 * (xs % 2), 4), :, lanes] = (
                    (dot(four, CW[g, 0]) * QSCALE).astype(BF16).reshape(4, 32, HALF)
                )

        return carry

    def a_recv(l):
        return remote(M.at[l], M.at[l], as_sem.at[0], ar_sem.at[l], par)

    lax.fori_loop(0, 4, level_step, 0)

    r = lax.broadcasted_iota(jnp.int32, (HALF, HALF), 0)
    t = lax.broadcasted_iota(jnp.int32, (HALF, HALF), 1)
    same = (r % 16) == (t % 16)
    low128 = low_half[:128]
    for pg in range(2):
        px = slice(16 * pg, 16 * pg + 16)
        parts = []
        for p in range(4):
            lanes = slice(128 * p, 128 * p + 128)
            qp = Q2[:, px, lanes].reshape(128, 128)
            kp = K2[:, px, lanes].reshape(HALF, 128)
            vp = V2[:, px, lanes].reshape(HALF, 128)
            zero = jnp.zeros_like(qp)
            qst = jnp.concatenate([jnp.where(low128, qp, zero), jnp.where(low128, zero, qp)], axis=0)
            s = jnp.where(same, dot_t(qst, kp), LOW)
            w = jnp.exp2(s - jnp.max(s, axis=1, keepdims=True))
            o = dot(w.astype(BF16), vp) / jnp.sum(w, axis=1, keepdims=True)
            parts.append(jnp.where(low128, o[:128], o[128:]).astype(BF16))
        total = dot(jnp.concatenate(parts[:2], axis=1), CO[0]) + dot(jnp.concatenate(parts[2:], axis=1), CO[1])
        res = M[pl.ds(8 * a, 8), px, :].reshape(128, D).astype(F32)
        out[:, px, :] = (res + total).astype(BF16).reshape(8, 16, D)

    for b in range(2):
        @pl.when(2 * c + b != i)
        def _():
            for cd in range(2):
                y_send(b, cd).wait_send()

    @pl.when(c == cs)
    def _():
        own_send.wait_send()

    for n in range(4):
        w_send[n].wait_send()
        w_fwd[n].wait_send()
    for jj in (j1, j2, j3):
        x_fwd(jj).wait_send()
        s1_fwd(jj).wait_send()
        s2_fwd(jj).wait_send()
    for n in range(16):
        @pl.when(jnp.logical_not(is_self(n)))
        def _():
            a_send(n).wait_send()


def shards(fields, window_qkv, window_out, level_embed, level_order, column_qkv, column_out):
    anywhere = pl.BlockSpec(memory_space=pl.ANY)
    dma = pltpu.SemaphoreType.DMA
    return pl.pallas_call(
        kernel,
        out_shape=jax.ShapeDtypeStruct((8, 32, D), BF16),
        in_specs=[anywhere] * 4 + [pl.BlockSpec(memory_space=pltpu.SMEM)] + [anywhere] * 2,
        out_specs=pl.BlockSpec(memory_space=pltpu.VMEM),
        scratch_shapes=[
            pltpu.VMEM((4, HALF, D), BF16),
            pltpu.VMEM((4, HALF, D), BF16),
            pltpu.VMEM((2, 3, D, HALF), BF16),
            pltpu.VMEM((2, HALF, D), BF16),
            pltpu.VMEM((2, 3, D, HALF), BF16),
            pltpu.VMEM((2, HALF, D), BF16),
            pltpu.VMEM((16, D), BF16),
            pltpu.VMEM((8, HALF, 128), BF16),
            pltpu.VMEM((2, HALF, 128), BF16),
            pltpu.VMEM((4, HALF, 128), BF16),
            pltpu.VMEM((8, HALF, 128), F32),
            pltpu.VMEM((8, HALF, 128), F32),
            pltpu.VMEM((8, 32, D), BF16),
            pltpu.VMEM((HALF, D), BF16),
            pltpu.VMEM((16, 8, D), F32),
            pltpu.VMEM((16, 32, D), BF16),
            pltpu.VMEM((16, 32, D), BF16),
            pltpu.VMEM((16, 32, D), BF16),
            pltpu.VMEM((16, 32, D), BF16),
            pltpu.VMEM((8, 32, D), BF16),
            dma((6,)), dma((2, 2)), dma((4,)), dma, dma, dma((4,)), dma((4,)),
            dma((4,)), dma((4,)), dma((4,)), dma((4,)), dma((4,)), dma((4,)), dma((4,)), dma((4,)),
            dma((16,)), dma((16,)),
        ],
        compiler_params=pltpu.CompilerParams(
            collective_id=0, has_side_effects=True, vmem_limit_bytes=40 * 1024 * 1024
        ),
        cost_estimate=pl.CostEstimate(flops=4_000_000_000, bytes_accessed=3_000_000, transcendentals=3_000_000),
    )(fields, window_qkv, window_out, level_embed, level_order, column_qkv, column_out)


def solution(mesh):
    return jax.shard_map(
        shards,
        mesh=mesh,
        in_specs=(
            P("lev", "pix", None),
            P(None, None, "head"),
            P("head", None),
            P(),
            P(),
            P(None, None, "head"),
            P("head", None),
        ),
        out_specs=P("head", ("pix", "lev"), None),
        check_vma=False,
    )
```

```python
import math

import jax
import jax.numpy as jnp
from jax import lax
from jax.experimental import pallas as pl
from jax.experimental.pallas import tpu as pltpu
from jax.sharding import PartitionSpec as P

MESH = pl.DeviceIdType.MESH
EPS = 1e-6
F32 = jnp.float32
BF16 = jnp.bfloat16
D = 512
HALF = 256
QSCALE = math.log2(math.e) / 8.0
LOW = -3.0e38


def normalize(values):
    return values * lax.rsqrt(jnp.mean(values * values, axis=-1, keepdims=True) + EPS)


def dot(a, b):
    return jnp.dot(a, b, preferred_element_type=F32)


def dot_t(a, b):
    return lax.dot_general(a, b, (((1,), (1,)), ((), ())), preferred_element_type=F32)


def quarter_of(xh, a, c):
    odd = xh % 2
    off = (1 - a) * (3 * c + (1 - c) * 2 * odd) + a * ((1 - c) + c * (2 - 2 * odd))
    return (xh + off) % 4


def quarter_owner(xh, q):
    odd = xh % 2
    off = (q - xh + 4) % 4
    is0 = jnp.where(off == 0, 1, 0)
    is1 = jnp.where(off == 1, 1, 0)
    is2 = jnp.where(off == 2, 1, 0)
    is3 = jnp.where(off == 3, 1, 0)
    a = is0 * odd + is1 + is2 * (1 - odd)
    c = is0 * odd + is2 * (1 - odd) + is3
    return a, c


def kernel(
    fields, wqkv, wout, embed, order, cqkv, cout,
    out,
    X, W, WO, CW, CO, EM, EB,
    QM, KS, VS, OA, MA, MID,
    M, K2, V2, Q2, PO, PR,
    loc_sem, ys_sem, yr_sem, own_s, own_r, xs_sem, xr_sem,
    s1s_sem, s1r_sem, s2s_sem, s2r_sem, ws_sem, wr_sem, wfs_sem, wfr_sem,
    as_sem, ar_sem, ps_sem, pr_sem,
):
    pix = lax.axis_index("pix")
    lev = lax.axis_index("lev")
    a = lax.axis_index("head")
    i = pix % 4
    base = pix - i
    c = lev % 2
    xh = lev // 2
    level = 4 * xh + i
    cs = i // 2
    q = quarter_of(xh, a, c)
    q_sib = quarter_of(xh, a, 1 - c)
    q_par = quarter_of(xh, 1 - a, c)
    q_dia = quarter_of(xh, 1 - a, 1 - c)
    sib = (pix, 2 * xh + 1 - c, a)
    par = (pix, lev, 1 - a)
    xn = (xh + c * (2 * a - 1) + 4) % 4
    wpar = (pix, 2 * xn + c, 1 - a)
    e = ((i + 1) // 2) % 2
    j1 = i + 1 - 2 * (i % 2)
    opposite = (i + 2) % 4
    mirror = 3 - i
    j2 = opposite * (1 - e) + mirror * e
    j3 = mirror * (1 - e) + opposite * e
    others = (j1, j2, j3)

    def rows(quarter):
        return pl.ds(pl.multiple_of(quarter * 64, 64), 64)

    def remote(src, dst, ss, rs, dev):
        return pltpu.make_async_remote_copy(
            src_ref=src, dst_ref=dst, send_sem=ss, recv_sem=rs,
            device_id=dev, device_id_type=MESH,
        )

    own_shard = pltpu.make_async_copy(fields.at[i % 2], X.at[i], loc_sem.at[5])

    @pl.when(c == cs)
    def _():
        own_shard.start()

    local = [
        pltpu.make_async_copy(wqkv, W.at[0], loc_sem.at[0]),
        pltpu.make_async_copy(wout, WO.at[0], loc_sem.at[1]),
        pltpu.make_async_copy(cqkv, CW.at[0], loc_sem.at[2]),
        pltpu.make_async_copy(cout, CO.at[0], loc_sem.at[3]),
        pltpu.make_async_copy(embed, EM, loc_sem.at[4]),
    ]
    for copy in local:
        copy.start()

    barrier = pltpu.get_barrier_semaphore()

    def greet(dev):
        pl.semaphore_signal(barrier, inc=1, device_id=dev, device_id_type=MESH)

    for jj in others:
        greet((base + jj, 2 * xh + cs, a))
    greet(sib)
    greet(par)
    greet(wpar)
    for l in range(16):
        xs = l // 4
        sa, sc = quarter_owner(jnp.int32(xs), xh)
        src = (base + l % 4, 2 * xs + sc, sa)
        is_me = (i == l % 4) & (xh == xs) & (sc == c) & (sa == a)

        @pl.when(jnp.logical_not(is_me))
        def _():
            greet(src)

    n_y = jnp.where(c == cs, 2, 4)
    n_self = jnp.where(q == xh, 1, 0)
    pl.semaphore_wait(barrier, n_y + 3 + 16 - n_self)

    def y_send(b, cd):
        t = 2 * c + b
        quarter = quarter_of(xh, a, cd)
        return remote(
            fields.at[b, rows(quarter)], X.at[i, rows(quarter)],
            ys_sem.at[b, cd], yr_sem.at[i], (base + t, 2 * xh + cd, a),
        )

    for b in range(2):
        @pl.when(2 * c + b != i)
        def _():
            for cd in range(2):
                y_send(b, cd).start()

    own_send = remote(fields.at[i % 2], X.at[i], own_s, own_r, sib)

    @pl.when(c == cs)
    def _():
        own_send.start()

    wrow = pl.ds(pl.multiple_of(c * HALF, HALF), HALF)
    worow = pl.ds(pl.multiple_of(c * 128, 128), 128)
    wrow2 = pl.ds(pl.multiple_of((1 - c) * HALF, HALF), HALF)
    worow2 = pl.ds(pl.multiple_of((1 - c) * 128, 128), 128)
    w_srcs = [wqkv.at[:, wrow], wout.at[worow], cqkv.at[:, wrow], cout.at[worow]]
    w_dsts = [W.at[1, :, wrow], WO.at[1, worow], CW.at[1, :, wrow], CO.at[1, worow]]
    w_rest = [W.at[1, :, wrow2], WO.at[1, worow2], CW.at[1, :, wrow2], CO.at[1, worow2]]
    w_send = [remote(s, d, ws_sem.at[n], wr_sem.at[n], wpar) for n, (s, d) in enumerate(zip(w_srcs, w_dsts))]
    w_fwd = [remote(d, d, wfs_sem.at[n], wfr_sem.at[n], sib) for n, d in enumerate(w_dsts)]
    w_fwd_in = [remote(d, d, wfs_sem.at[n], wfr_sem.at[n], sib) for n, d in enumerate(w_rest)]
    w_send[0].start()

    def x_fwd(j):
        return remote(X.at[j, rows(q)], X.at[j, rows(q)], xs_sem.at[j], xr_sem.at[j], par)

    def s1_fwd(j):
        return remote(X.at[j, rows(q)], X.at[j, rows(q)], s1s_sem.at[j], s1r_sem.at[j], sib)

    def s2_fwd(j):
        return remote(X.at[j, rows(q_par)], X.at[j, rows(q_par)], s2s_sem.at[j], s2r_sem.at[j], sib)

    def y_recv(j):
        return remote(X.at[j, rows(q)], X.at[j, rows(q)], ys_sem.at[0, 0], yr_sem.at[j], par)

    def x_recv(j):
        return remote(X.at[j, rows(q_par)], X.at[j, rows(q_par)], xs_sem.at[j], xr_sem.at[j], par)

    def s1_recv(j):
        return remote(X.at[j, rows(q_sib)], X.at[j, rows(q_sib)], s1s_sem.at[j], s1r_sem.at[j], sib)

    def s2_recv(j):
        return remote(X.at[j, rows(q_dia)], X.at[j, rows(q_dia)], s2s_sem.at[j], s2r_sem.at[j], sib)

    lane = lax.broadcasted_iota(jnp.int32, (HALF, 128), 1)
    low_half = lane < 64

    def normed(j):
        return normalize(X[j].astype(F32)).astype(BF16)

    def keys_values(n, g):
        k = dot(n, W[g, 1]).astype(BF16)
        v = dot(n, W[g, 2])
        ks = [k[:, :128], k[:, 128:]]
        vs = []
        for p in range(2):
            vp = v[:, 128 * p:128 * p + 128]
            vs.append(jnp.where(low_half, vp, 1.0).astype(BF16))
            vs.append(jnp.where(low_half, 1.0, vp).astype(BF16))
        return ks, vs

    def queries(nq, g):
        qs = dot(nq, W[g, 0]) * QSCALE
        for h in range(4):
            pair = qs[:, 128 * (h // 2):128 * (h // 2) + 128]
            keep = low_half if h % 2 == 0 else jnp.logical_not(low_half)
            QM[4 * g + h] = jnp.where(keep, pair, 0.0).astype(BF16)

    def attend(kv, g, first=False, last=False):
        ks, vs = kv
        heads = [4 * g + h for h in range(4)]
        qs = [QM[hh] for hh in heads]
        if not first:
            olds = [MA[hh] for hh in heads]
            sums = [OA[hh] for hh in heads]
        tops, news = [], []
        for h in range(4):
            s = dot_t(qs[h], ks[h // 2])
            top = jnp.max(s, axis=1, keepdims=True)
            top = jnp.broadcast_to(top, (HALF, 128)) if first else jnp.maximum(olds[h], top)
            w = jnp.concatenate(
                [jnp.exp2(s[:, :128] - top).astype(BF16), jnp.exp2(s[:, 128:] - top).astype(BF16)], axis=1
            )
            o = dot(w, vs[h])
            if not first:
                o = sums[h] * jnp.exp2(olds[h] - top) + o
            tops.append(top)
            news.append(o)
        if not last:
            for h in range(4):
                OA[heads[h]] = news[h]
                MA[heads[h]] = tops[h]
        return news

    @pl.when(c == cs)
    def _():
        own_shard.wait()

    @pl.when(c != cs)
    def _():
        own_send.wait_recv()

    local[0].wait()
    N_own = normed(i)
    ks, vs = keys_values(N_own, 0)
    for p in range(2):
        KS[p] = ks[p]
    for h in range(4):
        VS[h] = vs[h]

    for jj in others:
        y_recv(jj).wait_recv()
        x_fwd(jj).start()
        s1_fwd(jj).start()
    w_send[1].start()

    qrows = X[:, rows(q), :].reshape(HALF, D).astype(F32)
    queries(normalize(qrows).astype(BF16), 0)
    x_recv(j1).wait_recv()
    s2_fwd(j1).start()
    attend(([KS[p] for p in range(2)], [VS[h] for h in range(4)]), 0, first=True)
    x_recv(j2).wait_recv()
    s2_fwd(j2).start()
    w_send[0].wait_recv()
    w_fwd[0].start()
    s1_recv(j1).wait_recv()
    s2_recv(j1).wait_recv()
    attend(keys_values(normed(j1), 0), 0)
    x_recv(j3).wait_recv()
    s2_fwd(j3).start()
    w_send[2].start()
    w_send[3].start()
    w_fwd_in[0].wait_recv()
    qrows = X[:, rows(q), :].reshape(HALF, D).astype(F32)
    queries(normalize(qrows).astype(BF16), 1)
    attend(keys_values(normed(i), 1), 1, first=True)
    attend(keys_values(normed(j1), 1), 1)
    w_send[1].wait_recv()
    w_fwd[1].start()
    s1_recv(j2).wait_recv()
    s2_recv(j2).wait_recv()
    n = normed(j2)
    kv0 = keys_values(n, 0)
    kv1 = keys_values(n, 1)
    attend(kv0, 0)
    attend(kv1, 1)
    s1_recv(j3).wait_recv()
    s2_recv(j3).wait_recv()
    w_fwd_in[1].wait_recv()
    local[1].wait()
    n = normed(j3)
    kv0 = keys_values(n, 0)
    kv1 = keys_values(n, 1)
    sums = attend(kv0, 0, last=True) + attend(kv1, 1, last=True)

    att = []
    for p in range(4):
        oa, ob = sums[2 * p], sums[2 * p + 1]
        num = jnp.where(low_half, oa, ob)
        den = pltpu.roll(jnp.where(low_half, ob, oa), 64, 1)
        att.append((num / den).astype(BF16))
    qrows = X[:, rows(q), :].reshape(HALF, D).astype(F32)
    mid = qrows + dot(jnp.concatenate(att[:2], axis=1), WO[0]) + dot(jnp.concatenate(att[2:], axis=1), WO[1])
    MID[...] = mid.astype(BF16).reshape(16, 16, D)

    def a_send(k, r):
        j = (i + k) % 4
        n = 4 * j + r
        return remote(
            MID.at[n], M.at[level], as_sem.at[n], ar_sem.at[level],
            (base + j, 2 * q + r // 2, r % 2),
        )

    def is_self(r):
        return (q == xh) & (c == r // 2) & (a == r % 2)

    self_copy = pltpu.make_async_copy(MID.at[4 * i + 2 * c + a], M.at[level], loc_sem.at[5])

    @pl.when(q == xh)
    def _():
        self_copy.start()

    for k in range(4):
        for r in range(4):
            if k == 0:
                @pl.when(jnp.logical_not(is_self(r)))
                def _():
                    a_send(k, r).start()
            else:
                a_send(k, r).start()

    local[4].wait()
    row = lax.broadcasted_iota(jnp.int32, (16, 16), 0)
    col = lax.broadcasted_iota(jnp.int32, (16, 16), 1)
    target = jnp.zeros((16, 16), jnp.int32)
    for l in range(16):
        target = jnp.where(row == l, order[l], target)
    onehot = jnp.where(col == target, 1.0, 0.0).astype(BF16)
    EB[...] = jnp.broadcast_to(dot(onehot, EM[...]).reshape(16, 1, D), (16, 16, D))

    for n in range(2, 4):
        w_send[n].wait_recv()
        w_fwd[n].start()
    for n in range(2, 4):
        local[n].wait()
        w_fwd_in[n].wait_recv()

    def level_half(k):
        for m in range(8):
            l = 8 * k + m
            mine = (l == level) & (q == xh)

            @pl.when(mine)
            def _():
                self_copy.wait()

            @pl.when(jnp.logical_not(mine))
            def _():
                remote(M.at[l], M.at[l], as_sem.at[0], ar_sem.at[l], par).wait_recv()

        eight = pl.ds(8 * k, 8)
        n2 = normalize((M[eight].astype(F32) + EB[eight]).reshape(128, D)).astype(BF16)
        for g in range(2):
            K2[k, :, HALF * g:HALF * g + HALF] = dot(n2, CW[g, 1]).astype(BF16)
            V2[k, :, HALF * g:HALF * g + HALF] = dot(n2, CW[g, 2]).astype(BF16)
            Q2[k, :, HALF * g:HALF * g + HALF] = (dot(n2, CW[g, 0]) * QSCALE).astype(BF16)

    level_half(xh // 2)
    level_half(1 - xh // 2)

    r = lax.broadcasted_iota(jnp.int32, (HALF, HALF), 0)
    t = lax.broadcasted_iota(jnp.int32, (HALF, HALF), 1)
    same = (r % 16) == (t % 16)
    low128 = low_half[:128]

    def columns(k):
        parts = []
        for p in range(4):
            lanes = slice(128 * p, 128 * p + 128)
            qp = Q2[k, :, lanes]
            kp = K2[:, :, lanes].reshape(HALF, 128)
            vp = V2[:, :, lanes].reshape(HALF, 128)
            zero = jnp.zeros_like(qp)
            qst = jnp.concatenate([jnp.where(low128, qp, zero), jnp.where(low128, zero, qp)], axis=0)
            s = jnp.where(same, dot_t(qst, kp), LOW)
            w = jnp.exp2(s - jnp.max(s, axis=1, keepdims=True))
            o = dot(w.astype(BF16), vp) / jnp.sum(w, axis=1, keepdims=True)
            parts.append(jnp.where(low128, o[:128], o[128:]).astype(BF16))
        total = dot(jnp.concatenate(parts[:2], axis=1), CO[0]) + dot(jnp.concatenate(parts[2:], axis=1), CO[1])
        res = M[pl.ds(8 * k, 8)].reshape(128, D).astype(F32)
        return (res + total).astype(BF16).reshape(8, 16, D)

    PO[...] = columns(1 - a)
    last = remote(PO, PR, ps_sem, pr_sem, par)
    last.start()
    out[:, pl.ds(pl.multiple_of(16 * a, 16), 16), :] = columns(a)

    for b in range(2):
        @pl.when(2 * c + b != i)
        def _():
            for cd in range(2):
                y_send(b, cd).wait_send()

    @pl.when(c == cs)
    def _():
        own_send.wait_send()

    for n in range(4):
        w_send[n].wait_send()
        w_fwd[n].wait_send()
    for jj in others:
        x_fwd(jj).wait_send()
        s1_fwd(jj).wait_send()
        s2_fwd(jj).wait_send()
    for k in range(4):
        for r in range(4):
            if k == 0:
                @pl.when(jnp.logical_not(is_self(r)))
                def _():
                    a_send(k, r).wait_send()
            else:
                a_send(k, r).wait_send()
    last.wait_recv()
    out[:, pl.ds(pl.multiple_of(16 - 16 * a, 16), 16), :] = PR[...]
    last.wait_send()


def shards(fields, window_qkv, window_out, level_embed, level_order, column_qkv, column_out):
    anywhere = pl.BlockSpec(memory_space=pltpu.HBM)
    dma = pltpu.SemaphoreType.DMA
    return pl.pallas_call(
        kernel,
        out_shape=jax.ShapeDtypeStruct((8, 32, D), BF16),
        in_specs=[anywhere] * 4 + [pl.BlockSpec(memory_space=pltpu.SMEM)] + [anywhere] * 2,
        out_specs=pl.BlockSpec(memory_space=pltpu.VMEM),
        scratch_shapes=[
            pltpu.VMEM((4, HALF, D), BF16),
            pltpu.VMEM((2, 3, D, HALF), BF16),
            pltpu.VMEM((2, HALF, D), BF16),
            pltpu.VMEM((2, 3, D, HALF), BF16),
            pltpu.VMEM((2, HALF, D), BF16),
            pltpu.VMEM((16, D), BF16),
            pltpu.VMEM((16, 16, D), F32),
            pltpu.VMEM((8, HALF, 128), BF16),
            pltpu.VMEM((2, HALF, 128), BF16),
            pltpu.VMEM((4, HALF, 128), BF16),
            pltpu.VMEM((8, HALF, 128), F32),
            pltpu.VMEM((8, HALF, 128), F32),
            pltpu.VMEM((16, 16, D), BF16),
            pltpu.VMEM((16, 16, D), BF16),
            pltpu.VMEM((2, 128, D), BF16),
            pltpu.VMEM((2, 128, D), BF16),
            pltpu.VMEM((2, 128, D), BF16),
            pltpu.VMEM((8, 16, D), BF16),
            pltpu.VMEM((8, 16, D), BF16),
            dma((6,)), dma((2, 2)), dma((4,)), dma, dma, dma((4,)), dma((4,)),
            dma((4,)), dma((4,)), dma((4,)), dma((4,)), dma((4,)), dma((4,)), dma((4,)), dma((4,)),
            dma((16,)), dma((16,)), dma, dma,
        ],
        compiler_params=pltpu.CompilerParams(
            collective_id=0, has_side_effects=True, vmem_limit_bytes=60 * 1024 * 1024
        ),
        cost_estimate=pl.CostEstimate(flops=4_000_000_000, bytes_accessed=3_000_000, transcendentals=3_000_000),
    )(fields, window_qkv, window_out, level_embed, level_order, column_qkv, column_out)


def solution(mesh):
    return jax.shard_map(
        shards,
        mesh=mesh,
        in_specs=(
            P("lev", "pix", None),
            P(None, None, "head"),
            P("head", None),
            P(),
            P(),
            P(None, None, "head"),
            P("head", None),
        ),
        out_specs=P("head", ("pix", "lev"), None),
        check_vma=False,
    )
```

```python
import math

import jax
import jax.numpy as jnp
from jax import lax
from jax.experimental import pallas as pl
from jax.experimental.pallas import tpu as pltpu
from jax.sharding import PartitionSpec as P

MESH = pl.DeviceIdType.MESH
EPS = 1e-6
F32 = jnp.float32
BF16 = jnp.bfloat16
D = 512
HALF = 256
QSCALE = math.log2(math.e) / 8.0
LOW = -3.0e38


def normalize(values):
    return values * lax.rsqrt(jnp.mean(values * values, axis=-1, keepdims=True) + EPS)


def dot(a, b):
    return jnp.dot(a, b, preferred_element_type=F32)


def dot_t(a, b):
    return lax.dot_general(a, b, (((1,), (1,)), ((), ())), preferred_element_type=F32)


def quarter_of(xh, a, c):
    odd = xh % 2
    off = (1 - a) * (3 * c + (1 - c) * 2 * odd) + a * ((1 - c) + c * (2 - 2 * odd))
    return (xh + off) % 4


def kernel(
    fields, wqkv, wout, embed, order, cqkv, cout,
    out,
    X, W, WO, CW, CO, EM, EB,
    QM, KS, VS, OA, MA, MID,
    M, K2, V2, Q2, PO, PR,
    loc_sem, ys_sem, yr_sem, own_s, own_r, xs_sem, xr_sem,
    s1s_sem, s1r_sem, s2s_sem, s2r_sem, ws_sem, wr_sem, wfs_sem, wfr_sem,
    as_sem, ar_sem, ps_sem, pr_sem, round_sem,
):
    pix = lax.axis_index("pix")
    lev = lax.axis_index("lev")
    a = lax.axis_index("head")
    i = pix % 4
    base = pix - i
    c = lev % 2
    xh = lev // 2
    level = 4 * xh + i
    cs = i // 2
    q = quarter_of(xh, a, c)
    q_sib = quarter_of(xh, a, 1 - c)
    q_par = quarter_of(xh, 1 - a, c)
    q_dia = quarter_of(xh, 1 - a, 1 - c)
    sib = (pix, 2 * xh + 1 - c, a)
    par = (pix, lev, 1 - a)
    xn = (xh + c * (2 * a - 1) + 4) % 4
    wpar = (pix, 2 * xn + c, 1 - a)
    e = ((i + 1) // 2) % 2
    j1 = i + 1 - 2 * (i % 2)
    opposite = (i + 2) % 4
    mirror = 3 - i
    j2 = opposite * (1 - e) + mirror * e
    j3 = mirror * (1 - e) + opposite * e
    others = (j1, j2, j3)

    def rows(quarter):
        return pl.ds(pl.multiple_of(quarter * 64, 64), 64)

    def remote(src, dst, ss, rs, dev):
        return pltpu.make_async_remote_copy(
            src_ref=src, dst_ref=dst, send_sem=ss, recv_sem=rs,
            device_id=dev, device_id_type=MESH,
        )

    own_shard = pltpu.make_async_copy(fields.at[i % 2], X.at[i], loc_sem.at[5])

    @pl.when(c == cs)
    def _():
        own_shard.start()

    local = [
        pltpu.make_async_copy(wqkv, W.at[0], loc_sem.at[0]),
        pltpu.make_async_copy(wout, WO.at[0], loc_sem.at[1]),
        pltpu.make_async_copy(cqkv, CW.at[0], loc_sem.at[2]),
        pltpu.make_async_copy(cout, CO.at[0], loc_sem.at[3]),
        pltpu.make_async_copy(embed, EM, loc_sem.at[4]),
    ]
    for copy in local:
        copy.start()

    barrier = pltpu.get_barrier_semaphore()

    def greet(dev):
        pl.semaphore_signal(barrier, inc=1, device_id=dev, device_id_type=MESH)

    for jj in others:
        greet((base + jj, 2 * xh + cs, a))
    greet(sib)
    greet(par)
    greet(wpar)
    for jj in others:
        greet((base + jj, lev, a))
    pl.semaphore_wait(barrier, jnp.where(c == cs, 2, 4) + 6)

    def tell(n, devs):
        for dev in devs:
            pl.semaphore_signal(round_sem.at[n], inc=1, device_id=dev, device_id_type=MESH)

    def ring(wait, signal):
        @pl.when(c == 1)
        def _():
            if wait is not None:
                pl.semaphore_wait(round_sem.at[wait], 2)
            if signal is not None:
                tell(signal, (par, wpar))

    def y_send(b, cd):
        t = 2 * c + b
        quarter = quarter_of(xh, a, cd)
        return remote(
            fields.at[b, rows(quarter)], X.at[i, rows(quarter)],
            ys_sem.at[b, cd], yr_sem.at[i], (base + t, 2 * xh + cd, a),
        )

    for b in range(2):
        @pl.when(2 * c + b != i)
        def _():
            for cd in range(2):
                y_send(b, cd).start()

    own_send = remote(fields.at[i % 2], X.at[i], own_s, own_r, sib)

    @pl.when(c == cs)
    def _():
        own_send.start()

    W_FROM = [wqkv.at[0], wqkv.at[1], wqkv.at[2], wout, cqkv.at[0], cqkv.at[1], cqkv.at[2], cout]
    W_TO = [W.at[1, 0], W.at[1, 1], W.at[1, 2], WO.at[1], CW.at[1, 0], CW.at[1, 1], CW.at[1, 2], CO.at[1]]
    w_send = [remote(s, d, ws_sem.at[n], wr_sem.at[n], wpar) for n, (s, d) in enumerate(zip(W_FROM, W_TO))]
    w_fwd = [remote(d, d, wfs_sem.at[n], wfr_sem.at[n], sib) for n, d in enumerate(W_TO)]

    def w_start(*core_and_matrices):
        for core, matrices in enumerate(core_and_matrices):
            @pl.when(c == core)
            def _():
                for n in matrices:
                    w_send[n].start()

    def w_pass(*core_and_matrices):
        for core, matrices in enumerate(core_and_matrices):
            @pl.when(c == core)
            def _():
                for n in matrices:
                    w_send[n].wait_recv()
                    w_fwd[n].start()

    def w_take(*core_and_matrices):
        for core, matrices in enumerate(core_and_matrices):
            @pl.when(c != core)
            def _():
                for n in matrices:
                    w_fwd[n].wait_recv()

    w_start((1,), (0, 2, 5, 6, 7))

    tell(0, [(base + jj, lev, a) for jj in others])

    def x_fwd(j):
        return remote(X.at[j, rows(q)], X.at[j, rows(q)], xs_sem.at[j], xr_sem.at[j], par)

    def s1_fwd(j):
        return remote(X.at[j, rows(q)], X.at[j, rows(q)], s1s_sem.at[j], s1r_sem.at[j], sib)

    def s2_fwd(j):
        return remote(X.at[j, rows(q_par)], X.at[j, rows(q_par)], s2s_sem.at[j], s2r_sem.at[j], sib)

    def y_recv(j):
        return remote(X.at[j, rows(q)], X.at[j, rows(q)], ys_sem.at[0, 0], yr_sem.at[j], par)

    def x_recv(j):
        return remote(X.at[j, rows(q_par)], X.at[j, rows(q_par)], xs_sem.at[j], xr_sem.at[j], par)

    def s1_recv(j):
        return remote(X.at[j, rows(q_sib)], X.at[j, rows(q_sib)], s1s_sem.at[j], s1r_sem.at[j], sib)

    def s2_recv(j):
        return remote(X.at[j, rows(q_dia)], X.at[j, rows(q_dia)], s2s_sem.at[j], s2r_sem.at[j], sib)

    lane = lax.broadcasted_iota(jnp.int32, (HALF, 128), 1)
    low_half = lane < 64

    def normed(j):
        return normalize(X[j].astype(F32)).astype(BF16)

    def keys_values(n, g):
        k = dot(n, W[g, 1]).astype(BF16)
        v = dot(n, W[g, 2])
        ks = [k[:, :128], k[:, 128:]]
        vs = []
        for p in range(2):
            vp = v[:, 128 * p:128 * p + 128]
            vs.append(jnp.where(low_half, vp, 1.0).astype(BF16))
            vs.append(jnp.where(low_half, 1.0, vp).astype(BF16))
        return ks, vs

    def queries(nq, g):
        qs = dot(nq, W[g, 0]) * QSCALE
        for h in range(4):
            pair = qs[:, 128 * (h // 2):128 * (h // 2) + 128]
            keep = low_half if h % 2 == 0 else jnp.logical_not(low_half)
            QM[4 * g + h] = jnp.where(keep, pair, 0.0).astype(BF16)

    def attend(kv, g, first=False, last=False):
        ks, vs = kv
        heads = [4 * g + h for h in range(4)]
        qs = [QM[hh] for hh in heads]
        if not first:
            olds = [MA[hh] for hh in heads]
            sums = [OA[hh] for hh in heads]
        tops, news = [], []
        for h in range(4):
            s = dot_t(qs[h], ks[h // 2])
            top = jnp.max(s, axis=1, keepdims=True)
            top = jnp.broadcast_to(top, (HALF, 128)) if first else jnp.maximum(olds[h], top)
            w = jnp.concatenate(
                [jnp.exp2(s[:, :128] - top).astype(BF16), jnp.exp2(s[:, 128:] - top).astype(BF16)], axis=1
            )
            o = dot(w, vs[h])
            if not first:
                o = sums[h] * jnp.exp2(olds[h] - top) + o
            tops.append(top)
            news.append(o)
        if not last:
            for h in range(4):
                OA[heads[h]] = news[h]
                MA[heads[h]] = tops[h]
        return news

    @pl.when(c == cs)
    def _():
        own_shard.wait()

    @pl.when(c != cs)
    def _():
        own_send.wait_recv()

    local[0].wait()
    N_own = normed(i)
    ks, vs = keys_values(N_own, 0)
    for p in range(2):
        KS[p] = ks[p]
    for h in range(4):
        VS[h] = vs[h]

    pl.semaphore_wait(round_sem.at[0], 3)
    tell(1, (sib,))

    for jj in others:
        y_recv(jj).wait_recv()
        x_fwd(jj).start()
        s1_fwd(jj).start()
    w_start((3,))
    w_pass((1,), (0, 2))

    pl.semaphore_wait(round_sem.at[1], 1)
    ring(None, 2)
    qrows = X[:, rows(q), :].reshape(HALF, D).astype(F32)
    queries(normalize(qrows).astype(BF16), 0)
    x_recv(j1).wait_recv()
    s2_fwd(j1).start()
    attend(([KS[p] for p in range(2)], [VS[h] for h in range(4)]), 0, first=True)
    x_recv(j2).wait_recv()
    s2_fwd(j2).start()
    ring(2, 3)
    s1_recv(j1).wait_recv()
    s2_recv(j1).wait_recv()
    attend(keys_values(normed(j1), 0), 0)
    x_recv(j3).wait_recv()
    s2_fwd(j3).start()
    ring(3, 4)
    w_start((4,))
    w_take((1,), (0, 2))
    qrows = X[:, rows(q), :].reshape(HALF, D).astype(F32)
    queries(normalize(qrows).astype(BF16), 1)
    attend(keys_values(normed(i), 1), 1, first=True)
    attend(keys_values(normed(j1), 1), 1)
    ring(4, 5)
    s1_recv(j2).wait_recv()
    s2_recv(j2).wait_recv()
    n = normed(j2)
    kv0 = keys_values(n, 0)
    kv1 = keys_values(n, 1)
    attend(kv0, 0)
    attend(kv1, 1)
    ring(5, None)

    @pl.when(c == 1)
    def _():
        tell(6, (sib,))

    w_pass((3,))
    s1_recv(j3).wait_recv()
    s2_recv(j3).wait_recv()
    w_take((3,))
    local[1].wait()
    n = normed(j3)
    kv0 = keys_values(n, 0)
    kv1 = keys_values(n, 1)
    sums = attend(kv0, 0, last=True) + attend(kv1, 1, last=True)

    att = []
    for p in range(4):
        oa, ob = sums[2 * p], sums[2 * p + 1]
        num = jnp.where(low_half, oa, ob)
        den = pltpu.roll(jnp.where(low_half, ob, oa), 64, 1)
        att.append((num / den).astype(BF16))
    qrows = X[:, rows(q), :].reshape(HALF, D).astype(F32)
    mid = qrows + dot(jnp.concatenate(att[:2], axis=1), WO[0]) + dot(jnp.concatenate(att[2:], axis=1), WO[1])
    MID[...] = mid.astype(BF16).reshape(16, 16, D)

    def a_send(k, r):
        j = (i + k) % 4
        n = 4 * j + r
        return remote(
            MID.at[n], M.at[level], as_sem.at[n], ar_sem.at[level],
            (base + j, 2 * q + r // 2, r % 2),
        )

    def is_self(r):
        return (q == xh) & (c == r // 2) & (a == r % 2)

    self_copy = pltpu.make_async_copy(MID.at[4 * i + 2 * c + a], M.at[level], loc_sem.at[5])

    @pl.when(c == 0)
    def _():
        pl.semaphore_wait(round_sem.at[6], 1)

    @pl.when(q == xh)
    def _():
        self_copy.start()

    for k in range(4):
        for r in range(4):
            if k == 0:
                @pl.when(jnp.logical_not(is_self(r)))
                def _():
                    a_send(k, r).start()
            else:
                a_send(k, r).start()

    local[4].wait()
    row = lax.broadcasted_iota(jnp.int32, (16, 16), 0)
    col = lax.broadcasted_iota(jnp.int32, (16, 16), 1)
    target = jnp.zeros((16, 16), jnp.int32)
    for l in range(16):
        target = jnp.where(row == l, order[l], target)
    onehot = jnp.where(col == target, 1.0, 0.0).astype(BF16)
    EB[...] = jnp.broadcast_to(dot(onehot, EM[...]).reshape(16, 1, D), (16, 16, D))

    w_pass((4,), (5, 6, 7))
    w_take((4,), (5, 6, 7))
    for n in range(2, 4):
        local[n].wait()

    def level_half(k):
        for m in range(8):
            l = 8 * k + m
            mine = (l == level) & (q == xh)

            @pl.when(mine)
            def _():
                self_copy.wait()

            @pl.when(jnp.logical_not(mine))
            def _():
                remote(M.at[l], M.at[l], as_sem.at[0], ar_sem.at[l], par).wait_recv()

        eight = pl.ds(8 * k, 8)
        n2 = normalize((M[eight].astype(F32) + EB[eight]).reshape(128, D)).astype(BF16)
        for g in range(2):
            K2[k, :, HALF * g:HALF * g + HALF] = dot(n2, CW[g, 1]).astype(BF16)
            V2[k, :, HALF * g:HALF * g + HALF] = dot(n2, CW[g, 2]).astype(BF16)
            Q2[k, :, HALF * g:HALF * g + HALF] = (dot(n2, CW[g, 0]) * QSCALE).astype(BF16)

    level_half(xh // 2)
    level_half(1 - xh // 2)

    r = lax.broadcasted_iota(jnp.int32, (HALF, HALF), 0)
    t = lax.broadcasted_iota(jnp.int32, (HALF, HALF), 1)
    same = (r % 16) == (t % 16)
    low128 = low_half[:128]

    def columns(k):
        parts = []
        for p in range(4):
            lanes = slice(128 * p, 128 * p + 128)
            qp = Q2[k, :, lanes]
            kp = K2[:, :, lanes].reshape(HALF, 128)
            vp = V2[:, :, lanes].reshape(HALF, 128)
            zero = jnp.zeros_like(qp)
            qst = jnp.concatenate([jnp.where(low128, qp, zero), jnp.where(low128, zero, qp)], axis=0)
            s = jnp.where(same, dot_t(qst, kp), LOW)
            w = jnp.exp2(s - jnp.max(s, axis=1, keepdims=True))
            o = dot(w.astype(BF16), vp) / jnp.sum(w, axis=1, keepdims=True)
            parts.append(jnp.where(low128, o[:128], o[128:]).astype(BF16))
        total = dot(jnp.concatenate(parts[:2], axis=1), CO[0]) + dot(jnp.concatenate(parts[2:], axis=1), CO[1])
        res = M[pl.ds(8 * k, 8)].reshape(128, D).astype(F32)
        return (res + total).astype(BF16).reshape(8, 16, D)

    PO[...] = columns(1 - a)
    last = remote(PO, PR, ps_sem, pr_sem, par)
    last.start()
    out[:, pl.ds(pl.multiple_of(16 * a, 16), 16), :] = columns(a)

    for b in range(2):
        @pl.when(2 * c + b != i)
        def _():
            for cd in range(2):
                y_send(b, cd).wait_send()

    @pl.when(c == cs)
    def _():
        own_send.wait_send()

    for core, matrices in enumerate(((1, 3, 4), (0, 2, 5, 6, 7))):
        @pl.when(c == core)
        def _():
            for n in matrices:
                w_send[n].wait_send()
                w_fwd[n].wait_send()
    for jj in others:
        x_fwd(jj).wait_send()
        s1_fwd(jj).wait_send()
        s2_fwd(jj).wait_send()
    for k in range(4):
        for r in range(4):
            if k == 0:
                @pl.when(jnp.logical_not(is_self(r)))
                def _():
                    a_send(k, r).wait_send()
            else:
                a_send(k, r).wait_send()
    last.wait_recv()
    out[:, pl.ds(pl.multiple_of(16 - 16 * a, 16), 16), :] = PR[...]
    last.wait_send()


def shards(fields, window_qkv, window_out, level_embed, level_order, column_qkv, column_out):
    anywhere = pl.BlockSpec(memory_space=pltpu.HBM)
    dma = pltpu.SemaphoreType.DMA
    return pl.pallas_call(
        kernel,
        out_shape=jax.ShapeDtypeStruct((8, 32, D), BF16),
        in_specs=[anywhere] * 4 + [pl.BlockSpec(memory_space=pltpu.SMEM)] + [anywhere] * 2,
        out_specs=pl.BlockSpec(memory_space=pltpu.VMEM),
        scratch_shapes=[
            pltpu.VMEM((4, HALF, D), BF16),
            pltpu.VMEM((2, 3, D, HALF), BF16),
            pltpu.VMEM((2, HALF, D), BF16),
            pltpu.VMEM((2, 3, D, HALF), BF16),
            pltpu.VMEM((2, HALF, D), BF16),
            pltpu.VMEM((16, D), BF16),
            pltpu.VMEM((16, 16, D), F32),
            pltpu.VMEM((8, HALF, 128), BF16),
            pltpu.VMEM((2, HALF, 128), BF16),
            pltpu.VMEM((4, HALF, 128), BF16),
            pltpu.VMEM((8, HALF, 128), F32),
            pltpu.VMEM((8, HALF, 128), F32),
            pltpu.VMEM((16, 16, D), BF16),
            pltpu.VMEM((16, 16, D), BF16),
            pltpu.VMEM((2, 128, D), BF16),
            pltpu.VMEM((2, 128, D), BF16),
            pltpu.VMEM((2, 128, D), BF16),
            pltpu.VMEM((8, 16, D), BF16),
            pltpu.VMEM((8, 16, D), BF16),
            dma((6,)), dma((2, 2)), dma((4,)), dma, dma, dma((4,)), dma((4,)),
            dma((4,)), dma((4,)), dma((4,)), dma((4,)), dma((8,)), dma((8,)), dma((8,)), dma((8,)),
            dma((16,)), dma((16,)), dma, dma, pltpu.SemaphoreType.REGULAR((7,)),
        ],
        compiler_params=pltpu.CompilerParams(
            collective_id=0, has_side_effects=True, vmem_limit_bytes=60 * 1024 * 1024
        ),
        cost_estimate=pl.CostEstimate(flops=4_000_000_000, bytes_accessed=3_000_000, transcendentals=3_000_000),
    )(fields, window_qkv, window_out, level_embed, level_order, column_qkv, column_out)


def solution(mesh):
    return jax.shard_map(
        shards,
        mesh=mesh,
        in_specs=(
            P("lev", "pix", None),
            P(None, None, "head"),
            P("head", None),
            P(),
            P(),
            P(None, None, "head"),
            P("head", None),
        ),
        out_specs=P("head", ("pix", "lev"), None),
        check_vma=False,
    )
```

```python
import math

import jax
import jax.numpy as jnp
from jax import lax
from jax.experimental import pallas as pl
from jax.experimental.pallas import tpu as pltpu
from jax.sharding import PartitionSpec as P

MESH = pl.DeviceIdType.MESH
EPS = 1e-6
F32 = jnp.float32
BF16 = jnp.bfloat16
D = 512
HALF = 256
QSCALE = math.log2(math.e) / 8.0
LOW = -3.0e38


def normalize(values):
    return values * lax.rsqrt(jnp.mean(values * values, axis=-1, keepdims=True) + EPS)


def dot(a, b):
    return jnp.dot(a, b, preferred_element_type=F32)


def dot_t(a, b):
    return lax.dot_general(a, b, (((1,), (1,)), ((), ())), preferred_element_type=F32)


def quarter_of(xh, a, c):
    odd = xh % 2
    off = (1 - a) * (3 * c + (1 - c) * 2 * odd) + a * ((1 - c) + c * (2 - 2 * odd))
    return (xh + off) % 4


def kernel(
    fields, wqkv, wout, embed, order, cqkv, cout,
    out,
    X, W, WO, CW, CO, EM, EB,
    QM, KS, VS, OA, MA, MID,
    M, K2, V2, Q2, PO, PR,
    loc_sem, ys_sem, yr_sem, own_s, own_r, xs_sem, xr_sem,
    s1s_sem, s1r_sem, s2s_sem, s2r_sem, ws_sem, wr_sem, wfs_sem, wfr_sem,
    as_sem, ar_sem, ps_sem, pr_sem, round_sem,
):
    pix = lax.axis_index("pix")
    lev = lax.axis_index("lev")
    a = lax.axis_index("head")
    i = pix % 4
    base = pix - i
    c = lev % 2
    xh = lev // 2
    level = 4 * xh + i
    cs = i // 2
    q = quarter_of(xh, a, c)
    q_sib = quarter_of(xh, a, 1 - c)
    q_par = quarter_of(xh, 1 - a, c)
    q_dia = quarter_of(xh, 1 - a, 1 - c)
    sib = (pix, 2 * xh + 1 - c, a)
    par = (pix, lev, 1 - a)
    xn = (xh + c * (2 * a - 1) + 4) % 4
    wpar = (pix, 2 * xn + c, 1 - a)
    e = ((i + 1) // 2) % 2
    j1 = i + 1 - 2 * (i % 2)
    opposite = (i + 2) % 4
    mirror = 3 - i
    j2 = opposite * (1 - e) + mirror * e
    j3 = mirror * (1 - e) + opposite * e
    others = (j1, j2, j3)

    def rows(quarter):
        return pl.ds(pl.multiple_of(quarter * 64, 64), 64)

    def remote(src, dst, ss, rs, dev):
        return pltpu.make_async_remote_copy(
            src_ref=src, dst_ref=dst, send_sem=ss, recv_sem=rs,
            device_id=dev, device_id_type=MESH,
        )

    own_shard = pltpu.make_async_copy(fields.at[i % 2], X.at[i], loc_sem.at[5])

    @pl.when(c == cs)
    def _():
        own_shard.start()

    local = [
        pltpu.make_async_copy(wqkv, W.at[0], loc_sem.at[0]),
        pltpu.make_async_copy(wout, WO.at[0], loc_sem.at[1]),
        pltpu.make_async_copy(cqkv, CW.at[0], loc_sem.at[2]),
        pltpu.make_async_copy(cout, CO.at[0], loc_sem.at[3]),
        pltpu.make_async_copy(embed, EM, loc_sem.at[4]),
    ]
    for copy in local:
        copy.start()

    barrier = pltpu.get_barrier_semaphore()

    def greet(dev):
        pl.semaphore_signal(barrier, inc=1, device_id=dev, device_id_type=MESH)

    for jj in others:
        greet((base + jj, 2 * xh + cs, a))
    greet(sib)
    greet(par)
    greet(wpar)
    for jj in others:
        greet((base + jj, lev, a))
    pl.semaphore_wait(barrier, jnp.where(c == cs, 2, 4) + 6)

    def tell(n, devs):
        for dev in devs:
            pl.semaphore_signal(round_sem.at[n], inc=1, device_id=dev, device_id_type=MESH)

    def ring(wait, signal):
        @pl.when(c == 1)
        def _():
            if wait is not None:
                pl.semaphore_wait(round_sem.at[wait], 2)
            if signal is not None:
                tell(signal, (par, wpar))

    def y_send(b, cd):
        t = 2 * c + b
        quarter = quarter_of(xh, a, cd)
        return remote(
            fields.at[b, rows(quarter)], X.at[i, rows(quarter)],
            ys_sem.at[b, cd], yr_sem.at[i], (base + t, 2 * xh + cd, a),
        )

    for step in range(2):
        for b in range(2):
            @pl.when((2 * c + b != i) & ((i + step) % 2 == b))
            def _():
                for cd in range(2):
                    y_send(b, cd).start()

    own_send = remote(fields.at[i % 2], X.at[i], own_s, own_r, sib)

    @pl.when(c == cs)
    def _():
        own_send.start()

    W_FROM = [wqkv.at[0], wqkv.at[1], wqkv.at[2], wout, cqkv.at[0], cqkv.at[1], cqkv.at[2], cout]
    W_TO = [W.at[1, 0], W.at[1, 1], W.at[1, 2], WO.at[1], CW.at[1, 0], CW.at[1, 1], CW.at[1, 2], CO.at[1]]
    w_send = [remote(s, d, ws_sem.at[n], wr_sem.at[n], wpar) for n, (s, d) in enumerate(zip(W_FROM, W_TO))]
    w_fwd = [remote(d, d, wfs_sem.at[n], wfr_sem.at[n], sib) for n, d in enumerate(W_TO)]

    def w_start(*core_and_matrices):
        for core, matrices in enumerate(core_and_matrices):
            @pl.when(c == core)
            def _():
                for n in matrices:
                    w_send[n].start()

    def w_pass(*core_and_matrices):
        for core, matrices in enumerate(core_and_matrices):
            @pl.when(c == core)
            def _():
                for n in matrices:
                    w_send[n].wait_recv()
                    w_fwd[n].start()

    def w_take(*core_and_matrices):
        for core, matrices in enumerate(core_and_matrices):
            @pl.when(c != core)
            def _():
                for n in matrices:
                    w_fwd[n].wait_recv()

    w_start((1,), (0, 2, 5, 6, 7))

    tell(0, [(base + jj, lev, a) for jj in others])

    def x_fwd(j):
        return remote(X.at[j, rows(q)], X.at[j, rows(q)], xs_sem.at[j], xr_sem.at[j], par)

    def s1_fwd(j):
        return remote(X.at[j, rows(q)], X.at[j, rows(q)], s1s_sem.at[j], s1r_sem.at[j], sib)

    def s2_fwd(j):
        return remote(X.at[j, rows(q_par)], X.at[j, rows(q_par)], s2s_sem.at[j], s2r_sem.at[j], sib)

    def y_recv(j):
        return remote(X.at[j, rows(q)], X.at[j, rows(q)], ys_sem.at[0, 0], yr_sem.at[j], par)

    def x_recv(j):
        return remote(X.at[j, rows(q_par)], X.at[j, rows(q_par)], xs_sem.at[j], xr_sem.at[j], par)

    def s1_recv(j):
        return remote(X.at[j, rows(q_sib)], X.at[j, rows(q_sib)], s1s_sem.at[j], s1r_sem.at[j], sib)

    def s2_recv(j):
        return remote(X.at[j, rows(q_dia)], X.at[j, rows(q_dia)], s2s_sem.at[j], s2r_sem.at[j], sib)

    lane = lax.broadcasted_iota(jnp.int32, (HALF, 128), 1)
    low_half = lane < 64

    def normed(j):
        return normalize(X[j].astype(F32)).astype(BF16)

    def keys_values(n, g):
        k = dot(n, W[g, 1]).astype(BF16)
        v = dot(n, W[g, 2])
        ks = [k[:, :128], k[:, 128:]]
        vs = []
        for p in range(2):
            vp = v[:, 128 * p:128 * p + 128]
            vs.append(jnp.where(low_half, vp, 1.0).astype(BF16))
            vs.append(jnp.where(low_half, 1.0, vp).astype(BF16))
        return ks, vs

    def queries(nq, g):
        qs = dot(nq, W[g, 0]) * QSCALE
        for h in range(4):
            pair = qs[:, 128 * (h // 2):128 * (h // 2) + 128]
            keep = low_half if h % 2 == 0 else jnp.logical_not(low_half)
            QM[4 * g + h] = jnp.where(keep, pair, 0.0).astype(BF16)

    def attend(kv, g, first=False, last=False):
        ks, vs = kv
        heads = [4 * g + h for h in range(4)]
        qs = [QM[hh] for hh in heads]
        if not first:
            olds = [MA[hh] for hh in heads]
            sums = [OA[hh] for hh in heads]
        tops, news = [], []
        for h in range(4):
            s = dot_t(qs[h], ks[h // 2])
            top = jnp.max(s, axis=1, keepdims=True)
            top = jnp.broadcast_to(top, (HALF, 128)) if first else jnp.maximum(olds[h], top)
            w = jnp.concatenate(
                [jnp.exp2(s[:, :128] - top).astype(BF16), jnp.exp2(s[:, 128:] - top).astype(BF16)], axis=1
            )
            o = dot(w, vs[h])
            if not first:
                o = sums[h] * jnp.exp2(olds[h] - top) + o
            tops.append(top)
            news.append(o)
        if not last:
            for h in range(4):
                OA[heads[h]] = news[h]
                MA[heads[h]] = tops[h]
        return news

    @pl.when(c == cs)
    def _():
        own_shard.wait()

    @pl.when(c != cs)
    def _():
        own_send.wait_recv()

    local[0].wait()
    N_own = normed(i)
    ks, vs = keys_values(N_own, 0)
    for p in range(2):
        KS[p] = ks[p]
    for h in range(4):
        VS[h] = vs[h]

    pl.semaphore_wait(round_sem.at[0], 3)
    tell(1, (sib,))
    pl.semaphore_wait(round_sem.at[1], 1)
    ring(None, 2)

    for jj in others:
        y_recv(jj).wait_recv()
        x_fwd(jj).start()
        s1_fwd(jj).start()
    w_start((3,))
    w_pass((1,), (0, 2))
    ring(2, 3)

    qrows = X[:, rows(q), :].reshape(HALF, D).astype(F32)
    queries(normalize(qrows).astype(BF16), 0)
    x_recv(j1).wait_recv()
    s2_fwd(j1).start()
    attend(([KS[p] for p in range(2)], [VS[h] for h in range(4)]), 0, first=True)
    x_recv(j2).wait_recv()
    s2_fwd(j2).start()
    ring(3, 4)
    s1_recv(j1).wait_recv()
    s2_recv(j1).wait_recv()
    attend(keys_values(normed(j1), 0), 0)
    x_recv(j3).wait_recv()
    s2_fwd(j3).start()
    ring(4, 5)
    w_start((4,))
    w_take((1,), (0, 2))
    qrows = X[:, rows(q), :].reshape(HALF, D).astype(F32)
    queries(normalize(qrows).astype(BF16), 1)
    attend(keys_values(normed(i), 1), 1, first=True)
    attend(keys_values(normed(j1), 1), 1)
    ring(5, None)

    @pl.when(c == 1)
    def _():
        tell(6, (sib,))

    s1_recv(j2).wait_recv()
    s2_recv(j2).wait_recv()
    n = normed(j2)
    kv0 = keys_values(n, 0)
    kv1 = keys_values(n, 1)
    attend(kv0, 0)
    attend(kv1, 1)
    w_pass((3,))
    s1_recv(j3).wait_recv()
    s2_recv(j3).wait_recv()
    w_take((3,))
    local[1].wait()
    n = normed(j3)
    kv0 = keys_values(n, 0)
    kv1 = keys_values(n, 1)
    sums = attend(kv0, 0, last=True) + attend(kv1, 1, last=True)

    att = []
    for p in range(4):
        oa, ob = sums[2 * p], sums[2 * p + 1]
        num = jnp.where(low_half, oa, ob)
        den = pltpu.roll(jnp.where(low_half, ob, oa), 64, 1)
        att.append((num / den).astype(BF16))
    qrows = X[:, rows(q), :].reshape(HALF, D).astype(F32)
    mid = qrows + dot(jnp.concatenate(att[:2], axis=1), WO[0]) + dot(jnp.concatenate(att[2:], axis=1), WO[1])
    MID[...] = mid.astype(BF16).reshape(16, 16, D)

    def a_send(k, r):
        j = (i, j1, opposite, mirror)[k]
        n = 4 * j + r
        return remote(
            MID.at[n], M.at[level], as_sem.at[n], ar_sem.at[level],
            (base + j, 2 * q + r // 2, r % 2),
        )

    def is_self(r):
        return (q == xh) & (c == r // 2) & (a == r % 2)

    self_copy = pltpu.make_async_copy(MID.at[4 * i + 2 * c + a], M.at[level], loc_sem.at[5])

    @pl.when(c == 0)
    def _():
        pl.semaphore_wait(round_sem.at[6], 1)

    @pl.when(q == xh)
    def _():
        self_copy.start()

    for k in (3, 2, 1, 0):
        for r in range(4):
            if k == 0:
                @pl.when(jnp.logical_not(is_self(r)))
                def _():
                    a_send(k, r).start()
            else:
                a_send(k, r).start()

    local[4].wait()
    row = lax.broadcasted_iota(jnp.int32, (16, 16), 0)
    col = lax.broadcasted_iota(jnp.int32, (16, 16), 1)
    target = jnp.zeros((16, 16), jnp.int32)
    for l in range(16):
        target = jnp.where(row == l, order[l], target)
    onehot = jnp.where(col == target, 1.0, 0.0).astype(BF16)
    EB[...] = jnp.broadcast_to(dot(onehot, EM[...]).reshape(16, 1, D), (16, 16, D))

    w_pass((4,), (5, 6, 7))
    w_take((4,), (5, 6, 7))
    for n in range(2, 4):
        local[n].wait()

    def level_half(k):
        for m in range(8):
            l = 8 * k + m
            mine = (l == level) & (q == xh)

            @pl.when(mine)
            def _():
                self_copy.wait()

            @pl.when(jnp.logical_not(mine))
            def _():
                remote(M.at[l], M.at[l], as_sem.at[0], ar_sem.at[l], par).wait_recv()

        eight = pl.ds(8 * k, 8)
        n2 = normalize((M[eight].astype(F32) + EB[eight]).reshape(128, D)).astype(BF16)
        for g in range(2):
            K2[k, :, HALF * g:HALF * g + HALF] = dot(n2, CW[g, 1]).astype(BF16)
            V2[k, :, HALF * g:HALF * g + HALF] = dot(n2, CW[g, 2]).astype(BF16)
            Q2[k, :, HALF * g:HALF * g + HALF] = (dot(n2, CW[g, 0]) * QSCALE).astype(BF16)

    level_half(xh // 2)
    level_half(1 - xh // 2)

    r = lax.broadcasted_iota(jnp.int32, (HALF, HALF), 0)
    t = lax.broadcasted_iota(jnp.int32, (HALF, HALF), 1)
    same = (r % 16) == (t % 16)
    low128 = low_half[:128]

    def columns(k):
        parts = []
        for p in range(4):
            lanes = slice(128 * p, 128 * p + 128)
            qp = Q2[k, :, lanes]
            kp = K2[:, :, lanes].reshape(HALF, 128)
            vp = V2[:, :, lanes].reshape(HALF, 128)
            zero = jnp.zeros_like(qp)
            qst = jnp.concatenate([jnp.where(low128, qp, zero), jnp.where(low128, zero, qp)], axis=0)
            s = jnp.where(same, dot_t(qst, kp), LOW)
            w = jnp.exp2(s - jnp.max(s, axis=1, keepdims=True))
            o = dot(w.astype(BF16), vp) / jnp.sum(w, axis=1, keepdims=True)
            parts.append(jnp.where(low128, o[:128], o[128:]).astype(BF16))
        total = dot(jnp.concatenate(parts[:2], axis=1), CO[0]) + dot(jnp.concatenate(parts[2:], axis=1), CO[1])
        res = M[pl.ds(8 * k, 8)].reshape(128, D).astype(F32)
        return (res + total).astype(BF16).reshape(8, 16, D)

    PO[...] = columns(1 - a)
    last = remote(PO, PR, ps_sem, pr_sem, par)
    last.start()
    out[:, pl.ds(pl.multiple_of(16 * a, 16), 16), :] = columns(a)

    for b in range(2):
        @pl.when(2 * c + b != i)
        def _():
            for cd in range(2):
                y_send(b, cd).wait_send()

    @pl.when(c == cs)
    def _():
        own_send.wait_send()

    for core, matrices in enumerate(((1, 3, 4), (0, 2, 5, 6, 7))):
        @pl.when(c == core)
        def _():
            for n in matrices:
                w_send[n].wait_send()
                w_fwd[n].wait_send()
    for jj in others:
        x_fwd(jj).wait_send()
        s1_fwd(jj).wait_send()
        s2_fwd(jj).wait_send()
    for k in range(4):
        for r in range(4):
            if k == 0:
                @pl.when(jnp.logical_not(is_self(r)))
                def _():
                    a_send(k, r).wait_send()
            else:
                a_send(k, r).wait_send()
    last.wait_recv()
    out[:, pl.ds(pl.multiple_of(16 - 16 * a, 16), 16), :] = PR[...]
    last.wait_send()


def shards(fields, window_qkv, window_out, level_embed, level_order, column_qkv, column_out):
    anywhere = pl.BlockSpec(memory_space=pltpu.HBM)
    dma = pltpu.SemaphoreType.DMA
    return pl.pallas_call(
        kernel,
        out_shape=jax.ShapeDtypeStruct((8, 32, D), BF16),
        in_specs=[anywhere] * 4 + [pl.BlockSpec(memory_space=pltpu.SMEM)] + [anywhere] * 2,
        out_specs=pl.BlockSpec(memory_space=pltpu.VMEM),
        scratch_shapes=[
            pltpu.VMEM((4, HALF, D), BF16),
            pltpu.VMEM((2, 3, D, HALF), BF16),
            pltpu.VMEM((2, HALF, D), BF16),
            pltpu.VMEM((2, 3, D, HALF), BF16),
            pltpu.VMEM((2, HALF, D), BF16),
            pltpu.VMEM((16, D), BF16),
            pltpu.VMEM((16, 16, D), F32),
            pltpu.VMEM((8, HALF, 128), BF16),
            pltpu.VMEM((2, HALF, 128), BF16),
            pltpu.VMEM((4, HALF, 128), BF16),
            pltpu.VMEM((8, HALF, 128), F32),
            pltpu.VMEM((8, HALF, 128), F32),
            pltpu.VMEM((16, 16, D), BF16),
            pltpu.VMEM((16, 16, D), BF16),
            pltpu.VMEM((2, 128, D), BF16),
            pltpu.VMEM((2, 128, D), BF16),
            pltpu.VMEM((2, 128, D), BF16),
            pltpu.VMEM((8, 16, D), BF16),
            pltpu.VMEM((8, 16, D), BF16),
            dma((6,)), dma((2, 2)), dma((4,)), dma, dma, dma((4,)), dma((4,)),
            dma((4,)), dma((4,)), dma((4,)), dma((4,)), dma((8,)), dma((8,)), dma((8,)), dma((8,)),
            dma((16,)), dma((16,)), dma, dma, pltpu.SemaphoreType.REGULAR((7,)),
        ],
        compiler_params=pltpu.CompilerParams(
            collective_id=0, has_side_effects=True, vmem_limit_bytes=60 * 1024 * 1024
        ),
        cost_estimate=pl.CostEstimate(flops=4_000_000_000, bytes_accessed=3_000_000, transcendentals=3_000_000),
    )(fields, window_qkv, window_out, level_embed, level_order, column_qkv, column_out)


def solution(mesh):
    return jax.shard_map(
        shards,
        mesh=mesh,
        in_specs=(
            P("lev", "pix", None),
            P(None, None, "head"),
            P("head", None),
            P(),
            P(),
            P(None, None, "head"),
            P("head", None),
        ),
        out_specs=P("head", ("pix", "lev"), None),
        check_vma=False,
    )
```

```python
import math

import jax
import jax.numpy as jnp
from jax import lax
from jax.experimental import pallas as pl
from jax.experimental.pallas import tpu as pltpu
from jax.sharding import PartitionSpec as P

MESH = pl.DeviceIdType.MESH
EPS = 1e-6
F32 = jnp.float32
BF16 = jnp.bfloat16
D = 512
HALF = 256
QSCALE = math.log2(math.e) / 8.0
LOW = -3.0e38


def normalize(values):
    return values * lax.rsqrt(jnp.mean(values * values, axis=-1, keepdims=True) + EPS)


def dot(a, b):
    return jnp.dot(a, b, preferred_element_type=F32)


def dot_t(a, b):
    return lax.dot_general(a, b, (((1,), (1,)), ((), ())), preferred_element_type=F32)


def quarter_of(xh, a, c):
    odd = xh % 2
    off = (1 - a) * (3 * c + (1 - c) * 2 * odd) + a * ((1 - c) + c * (2 - 2 * odd))
    return (xh + off) % 4


def kernel(
    fields, wqkv, wout, embed, order, cqkv, cout,
    out,
    X, W, WO, CW, CO, EM, EB,
    QM, KS, VS, OA, MA, MID,
    M, K2, V2, Q2, PO, PR,
    loc_sem, ys_sem, yr_sem, own_s, own_r, xs_sem, xr_sem,
    s1s_sem, s1r_sem, s2s_sem, s2r_sem, ws_sem, wr_sem, wfs_sem, wfr_sem,
    as_sem, ar_sem, ps_sem, pr_sem, round_sem,
):
    pix = lax.axis_index("pix")
    lev = lax.axis_index("lev")
    a = lax.axis_index("head")
    i = pix % 4
    base = pix - i
    c = lev % 2
    xh = lev // 2
    level = 4 * xh + i
    cs = i // 2
    q = quarter_of(xh, a, c)
    q_sib = quarter_of(xh, a, 1 - c)
    q_par = quarter_of(xh, 1 - a, c)
    q_dia = quarter_of(xh, 1 - a, 1 - c)
    sib = (pix, 2 * xh + 1 - c, a)
    par = (pix, lev, 1 - a)
    xn = (xh + c * (2 * a - 1) + 4) % 4
    wpar = (pix, 2 * xn + c, 1 - a)
    e = ((i + 1) // 2) % 2
    j1 = i + 1 - 2 * (i % 2)
    opposite = (i + 2) % 4
    mirror = 3 - i
    j2 = opposite * (1 - e) + mirror * e
    j3 = mirror * (1 - e) + opposite * e
    others = (j1, j2, j3)

    def rows(quarter):
        return pl.ds(pl.multiple_of(quarter * 64, 64), 64)

    def remote(src, dst, ss, rs, dev):
        return pltpu.make_async_remote_copy(
            src_ref=src, dst_ref=dst, send_sem=ss, recv_sem=rs,
            device_id=dev, device_id_type=MESH,
        )

    own_shard = pltpu.make_async_copy(fields.at[i % 2], X.at[i], loc_sem.at[5])

    @pl.when(c == cs)
    def _():
        own_shard.start()

    local = [
        pltpu.make_async_copy(wqkv, W.at[0], loc_sem.at[0]),
        pltpu.make_async_copy(wout, WO.at[0], loc_sem.at[1]),
        pltpu.make_async_copy(cqkv, CW.at[0], loc_sem.at[2]),
        pltpu.make_async_copy(cout, CO.at[0], loc_sem.at[3]),
        pltpu.make_async_copy(embed, EM, loc_sem.at[4]),
    ]
    for copy in local:
        copy.start()

    barrier = pltpu.get_barrier_semaphore()

    def greet(dev):
        pl.semaphore_signal(barrier, inc=1, device_id=dev, device_id_type=MESH)

    for jj in others:
        greet((base + jj, 2 * xh + cs, a))
    greet(sib)
    greet(par)
    greet(wpar)
    for jj in others:
        greet((base + jj, lev, a))
    pl.semaphore_wait(barrier, jnp.where(c == cs, 2, 4) + 6)

    def tell(n, devs):
        for dev in devs:
            pl.semaphore_signal(round_sem.at[n], inc=1, device_id=dev, device_id_type=MESH)

    def ring(wait, signal):
        @pl.when(c == 1)
        def _():
            if wait is not None:
                pl.semaphore_wait(round_sem.at[wait], 2)
            if signal is not None:
                tell(signal, (par, wpar))

    def y_send(b, cd):
        t = 2 * c + b
        quarter = quarter_of(xh, a, cd)
        return remote(
            fields.at[b, rows(quarter)], X.at[i, rows(quarter)],
            ys_sem.at[b, cd], yr_sem.at[i], (base + t, 2 * xh + cd, a),
        )

    for step in range(2):
        for b in range(2):
            @pl.when((2 * c + b != i) & ((i + step) % 2 == b))
            def _():
                for cd in range(2):
                    y_send(b, cd).start()

    own_send = remote(fields.at[i % 2], X.at[i], own_s, own_r, sib)

    @pl.when(c == cs)
    def _():
        own_send.start()

    W_FROM = [wqkv.at[0], wqkv.at[1], wqkv.at[2], wout, cqkv.at[0], cqkv.at[1], cqkv.at[2], cout]
    W_TO = [W.at[1, 0], W.at[1, 1], W.at[1, 2], WO.at[1], CW.at[1, 0], CW.at[1, 1], CW.at[1, 2], CO.at[1]]
    w_send = [remote(s, d, ws_sem.at[n], wr_sem.at[n], wpar) for n, (s, d) in enumerate(zip(W_FROM, W_TO))]
    w_fwd = [remote(d, d, wfs_sem.at[n], wfr_sem.at[n], sib) for n, d in enumerate(W_TO)]

    def w_start(*core_and_matrices):
        for core, matrices in enumerate(core_and_matrices):
            @pl.when(c == core)
            def _():
                for n in matrices:
                    w_send[n].start()

    def w_pass(*core_and_matrices):
        for core, matrices in enumerate(core_and_matrices):
            @pl.when(c == core)
            def _():
                for n in matrices:
                    w_send[n].wait_recv()
                    w_fwd[n].start()

    def w_take(*core_and_matrices):
        for core, matrices in enumerate(core_and_matrices):
            @pl.when(c != core)
            def _():
                for n in matrices:
                    w_fwd[n].wait_recv()

    w_start((1,), (0, 2, 5, 6, 7))

    tell(0, [(base + jj, lev, a) for jj in others])

    def x_fwd(j):
        return remote(X.at[j, rows(q)], X.at[j, rows(q)], xs_sem.at[j], xr_sem.at[j], par)

    def s1_fwd(j):
        return remote(X.at[j, rows(q)], X.at[j, rows(q)], s1s_sem.at[j], s1r_sem.at[j], sib)

    def s2_fwd(j):
        return remote(X.at[j, rows(q_par)], X.at[j, rows(q_par)], s2s_sem.at[j], s2r_sem.at[j], sib)

    def y_recv(j):
        return remote(X.at[j, rows(q)], X.at[j, rows(q)], ys_sem.at[0, 0], yr_sem.at[j], par)

    def x_recv(j):
        return remote(X.at[j, rows(q_par)], X.at[j, rows(q_par)], xs_sem.at[j], xr_sem.at[j], par)

    def s1_recv(j):
        return remote(X.at[j, rows(q_sib)], X.at[j, rows(q_sib)], s1s_sem.at[j], s1r_sem.at[j], sib)

    def s2_recv(j):
        return remote(X.at[j, rows(q_dia)], X.at[j, rows(q_dia)], s2s_sem.at[j], s2r_sem.at[j], sib)

    lane = lax.broadcasted_iota(jnp.int32, (HALF, 128), 1)
    low_half = lane < 64

    def normed(j):
        return normalize(X[j].astype(F32)).astype(BF16)

    def keys_values(n, g):
        k = dot(n, W[g, 1]).astype(BF16)
        v = dot(n, W[g, 2])
        ks = [k[:, :128], k[:, 128:]]
        vs = []
        for p in range(2):
            vp = v[:, 128 * p:128 * p + 128]
            vs.append(jnp.where(low_half, vp, 1.0).astype(BF16))
            vs.append(jnp.where(low_half, 1.0, vp).astype(BF16))
        return ks, vs

    def queries(nq, g):
        qs = dot(nq, W[g, 0]) * QSCALE
        for h in range(4):
            pair = qs[:, 128 * (h // 2):128 * (h // 2) + 128]
            keep = low_half if h % 2 == 0 else jnp.logical_not(low_half)
            QM[4 * g + h] = jnp.where(keep, pair, 0.0).astype(BF16)

    def attend(kv, g, first=False, last=False):
        ks, vs = kv
        heads = [4 * g + h for h in range(4)]
        qs = [QM[hh] for hh in heads]
        if not first:
            olds = [MA[hh] for hh in heads]
            sums = [OA[hh] for hh in heads]
        tops, news = [], []
        for h in range(4):
            s = dot_t(qs[h], ks[h // 2])
            top = jnp.max(s, axis=1, keepdims=True)
            top = jnp.broadcast_to(top, (HALF, 128)) if first else jnp.maximum(olds[h], top)
            w = jnp.concatenate(
                [jnp.exp2(s[:, :128] - top).astype(BF16), jnp.exp2(s[:, 128:] - top).astype(BF16)], axis=1
            )
            o = dot(w, vs[h])
            if not first:
                o = sums[h] * jnp.exp2(olds[h] - top) + o
            tops.append(top)
            news.append(o)
        if not last:
            for h in range(4):
                OA[heads[h]] = news[h]
                MA[heads[h]] = tops[h]
        return news

    @pl.when(c == cs)
    def _():
        own_shard.wait()

    @pl.when(c != cs)
    def _():
        own_send.wait_recv()

    local[0].wait()
    N_own = normed(i)
    ks, vs = keys_values(N_own, 0)
    for p in range(2):
        KS[p] = ks[p]
    for h in range(4):
        VS[h] = vs[h]

    pl.semaphore_wait(round_sem.at[0], 3)
    tell(1, (sib,))
    pl.semaphore_wait(round_sem.at[1], 1)
    ring(None, 2)

    for jj in others:
        y_recv(jj).wait_recv()
        x_fwd(jj).start()
        s1_fwd(jj).start()
    w_start((3,))
    ring(2, 3)

    qrows = X[:, rows(q), :].reshape(HALF, D).astype(F32)
    queries(normalize(qrows).astype(BF16), 0)
    x_recv(j1).wait_recv()
    s2_fwd(j1).start()
    attend(([KS[p] for p in range(2)], [VS[h] for h in range(4)]), 0, first=True)
    w_pass((1,), (0, 2))
    x_recv(j2).wait_recv()
    s2_fwd(j2).start()
    ring(3, 4)
    s1_recv(j1).wait_recv()
    s2_recv(j1).wait_recv()
    attend(keys_values(normed(j1), 0), 0)
    x_recv(j3).wait_recv()
    s2_fwd(j3).start()
    ring(4, 5)
    w_start((4,))
    w_take((1,), (0, 2))
    qrows = X[:, rows(q), :].reshape(HALF, D).astype(F32)
    queries(normalize(qrows).astype(BF16), 1)
    attend(keys_values(normed(i), 1), 1, first=True)
    attend(keys_values(normed(j1), 1), 1)
    ring(5, None)

    @pl.when(c == 1)
    def _():
        tell(6, (sib,))

    s1_recv(j2).wait_recv()
    s2_recv(j2).wait_recv()
    n = normed(j2)
    kv0 = keys_values(n, 0)
    kv1 = keys_values(n, 1)
    attend(kv0, 0)
    attend(kv1, 1)
    w_pass((3,))
    s1_recv(j3).wait_recv()
    s2_recv(j3).wait_recv()
    w_take((3,))
    local[1].wait()
    n = normed(j3)
    kv0 = keys_values(n, 0)
    kv1 = keys_values(n, 1)
    sums = attend(kv0, 0, last=True) + attend(kv1, 1, last=True)

    att = []
    for p in range(4):
        oa, ob = sums[2 * p], sums[2 * p + 1]
        num = jnp.where(low_half, oa, ob)
        den = pltpu.roll(jnp.where(low_half, ob, oa), 64, 1)
        att.append((num / den).astype(BF16))
    qrows = X[:, rows(q), :].reshape(HALF, D).astype(F32)
    mid = qrows + dot(jnp.concatenate(att[:2], axis=1), WO[0]) + dot(jnp.concatenate(att[2:], axis=1), WO[1])
    MID[...] = mid.astype(BF16).reshape(16, 16, D)

    def a_send(k, r):
        j = (i, j1, opposite, mirror)[k]
        n = 4 * j + r
        return remote(
            MID.at[n], M.at[level], as_sem.at[n], ar_sem.at[level],
            (base + j, 2 * q + r // 2, r % 2),
        )

    def is_self(r):
        return (q == xh) & (c == r // 2) & (a == r % 2)

    self_copy = pltpu.make_async_copy(MID.at[4 * i + 2 * c + a], M.at[level], loc_sem.at[5])

    @pl.when(c == 0)
    def _():
        pl.semaphore_wait(round_sem.at[6], 1)

    @pl.when(q == xh)
    def _():
        self_copy.start()

    for k in (3, 2, 1, 0):
        for r in range(4):
            if k == 0:
                @pl.when(jnp.logical_not(is_self(r)))
                def _():
                    a_send(k, r).start()
            else:
                a_send(k, r).start()

    local[4].wait()
    row = lax.broadcasted_iota(jnp.int32, (16, 16), 0)
    col = lax.broadcasted_iota(jnp.int32, (16, 16), 1)
    target = jnp.zeros((16, 16), jnp.int32)
    for l in range(16):
        target = jnp.where(row == l, order[l], target)
    onehot = jnp.where(col == target, 1.0, 0.0).astype(BF16)
    EB[...] = jnp.broadcast_to(dot(onehot, EM[...]).reshape(16, 1, D), (16, 16, D))

    w_pass((4,), (5, 6, 7))
    w_take((4,), (5, 6, 7))
    for n in range(2, 4):
        local[n].wait()

    def level_half(k):
        for m in range(8):
            l = 8 * k + m
            mine = (l == level) & (q == xh)

            @pl.when(mine)
            def _():
                self_copy.wait()

            @pl.when(jnp.logical_not(mine))
            def _():
                remote(M.at[l], M.at[l], as_sem.at[0], ar_sem.at[l], par).wait_recv()

        eight = pl.ds(8 * k, 8)
        n2 = normalize((M[eight].astype(F32) + EB[eight]).reshape(128, D)).astype(BF16)
        for g in range(2):
            K2[k, :, HALF * g:HALF * g + HALF] = dot(n2, CW[g, 1]).astype(BF16)
            V2[k, :, HALF * g:HALF * g + HALF] = dot(n2, CW[g, 2]).astype(BF16)
            Q2[k, :, HALF * g:HALF * g + HALF] = (dot(n2, CW[g, 0]) * QSCALE).astype(BF16)

    level_half(xh // 2)
    level_half(1 - xh // 2)

    r = lax.broadcasted_iota(jnp.int32, (HALF, HALF), 0)
    t = lax.broadcasted_iota(jnp.int32, (HALF, HALF), 1)
    same = (r % 16) == (t % 16)
    low128 = low_half[:128]

    def columns(k):
        parts = []
        for p in range(4):
            lanes = slice(128 * p, 128 * p + 128)
            qp = Q2[k, :, lanes]
            kp = K2[:, :, lanes].reshape(HALF, 128)
            vp = V2[:, :, lanes].reshape(HALF, 128)
            zero = jnp.zeros_like(qp)
            qst = jnp.concatenate([jnp.where(low128, qp, zero), jnp.where(low128, zero, qp)], axis=0)
            s = jnp.where(same, dot_t(qst, kp), LOW)
            w = jnp.exp2(s - jnp.max(s, axis=1, keepdims=True))
            o = dot(w.astype(BF16), vp) / jnp.sum(w, axis=1, keepdims=True)
            parts.append(jnp.where(low128, o[:128], o[128:]).astype(BF16))
        total = dot(jnp.concatenate(parts[:2], axis=1), CO[0]) + dot(jnp.concatenate(parts[2:], axis=1), CO[1])
        res = M[pl.ds(8 * k, 8)].reshape(128, D).astype(F32)
        return (res + total).astype(BF16).reshape(8, 16, D)

    PO[...] = columns(1 - a)
    last = remote(PO, PR, ps_sem, pr_sem, par)
    last.start()
    out[:, pl.ds(pl.multiple_of(16 * a, 16), 16), :] = columns(a)

    for b in range(2):
        @pl.when(2 * c + b != i)
        def _():
            for cd in range(2):
                y_send(b, cd).wait_send()

    @pl.when(c == cs)
    def _():
        own_send.wait_send()

    for core, matrices in enumerate(((1, 3, 4), (0, 2, 5, 6, 7))):
        @pl.when(c == core)
        def _():
            for n in matrices:
                w_send[n].wait_send()
                w_fwd[n].wait_send()
    for jj in others:
        x_fwd(jj).wait_send()
        s1_fwd(jj).wait_send()
        s2_fwd(jj).wait_send()
    for k in range(4):
        for r in range(4):
            if k == 0:
                @pl.when(jnp.logical_not(is_self(r)))
                def _():
                    a_send(k, r).wait_send()
            else:
                a_send(k, r).wait_send()
    last.wait_recv()
    out[:, pl.ds(pl.multiple_of(16 - 16 * a, 16), 16), :] = PR[...]
    last.wait_send()


def shards(fields, window_qkv, window_out, level_embed, level_order, column_qkv, column_out):
    anywhere = pl.BlockSpec(memory_space=pltpu.HBM)
    dma = pltpu.SemaphoreType.DMA
    return pl.pallas_call(
        kernel,
        out_shape=jax.ShapeDtypeStruct((8, 32, D), BF16),
        in_specs=[anywhere] * 4 + [pl.BlockSpec(memory_space=pltpu.SMEM)] + [anywhere] * 2,
        out_specs=pl.BlockSpec(memory_space=pltpu.VMEM),
        scratch_shapes=[
            pltpu.VMEM((4, HALF, D), BF16),
            pltpu.VMEM((2, 3, D, HALF), BF16),
            pltpu.VMEM((2, HALF, D), BF16),
            pltpu.VMEM((2, 3, D, HALF), BF16),
            pltpu.VMEM((2, HALF, D), BF16),
            pltpu.VMEM((16, D), BF16),
            pltpu.VMEM((16, 16, D), F32),
            pltpu.VMEM((8, HALF, 128), BF16),
            pltpu.VMEM((2, HALF, 128), BF16),
            pltpu.VMEM((4, HALF, 128), BF16),
            pltpu.VMEM((8, HALF, 128), F32),
            pltpu.VMEM((8, HALF, 128), F32),
            pltpu.VMEM((16, 16, D), BF16),
            pltpu.VMEM((16, 16, D), BF16),
            pltpu.VMEM((2, 128, D), BF16),
            pltpu.VMEM((2, 128, D), BF16),
            pltpu.VMEM((2, 128, D), BF16),
            pltpu.VMEM((8, 16, D), BF16),
            pltpu.VMEM((8, 16, D), BF16),
            dma((6,)), dma((2, 2)), dma((4,)), dma, dma, dma((4,)), dma((4,)),
            dma((4,)), dma((4,)), dma((4,)), dma((4,)), dma((8,)), dma((8,)), dma((8,)), dma((8,)),
            dma((16,)), dma((16,)), dma, dma, pltpu.SemaphoreType.REGULAR((7,)),
        ],
        compiler_params=pltpu.CompilerParams(
            collective_id=0, has_side_effects=True, vmem_limit_bytes=60 * 1024 * 1024
        ),
        cost_estimate=pl.CostEstimate(flops=4_000_000_000, bytes_accessed=3_000_000, transcendentals=3_000_000),
    )(fields, window_qkv, window_out, level_embed, level_order, column_qkv, column_out)


def solution(mesh):
    return jax.shard_map(
        shards,
        mesh=mesh,
        in_specs=(
            P("lev", "pix", None),
            P(None, None, "head"),
            P("head", None),
            P(),
            P(),
            P(None, None, "head"),
            P("head", None),
        ),
        out_specs=P("head", ("pix", "lev"), None),
        check_vma=False,
    )
```
